256 devices in a mesh: seq: 64 (over z, x, y_hi), tp: 4 (over y_lo, core).
Axes of the slice: x: 4, y: 4 (y_hi: 2, y_lo: 2; y = y_hi * 2 + y_lo), z: 8, core: 2. Of those that a mesh axis runs over, the one named last changes fastest.
Arguments:
- q_gate: bfloat16 [8192, 4096], P(('seq', 'tp')), may hold values from -6 to 6
- key_in: bfloat16 [8192, 4096], P(('seq', 'tp')), may hold values from -6 to 6
- value_in: bfloat16 [8192, 4096], P(('seq', 'tp')), may hold values from -6 to 6
- out_grad: bfloat16 [8192, 4096], P(('seq', 'tp')), may hold values from -6 to 6
- mr_filter: float32 [4096, 128], P('tp'), may hold values from -0.5 to 0.5
- residues: float32 [4096, 16], P('tp'), may hold values from -1.5 to 1.5
- decay_rates: float32 [4096, 16], P('tp'), may hold values from 6.1035157e-06 to 0.05
Outputs:
- q_grad: bfloat16 [8192, 4096], P('seq', 'tp')
- key_grad: bfloat16 [8192, 4096], P('seq', 'tp')
- value_grad: bfloat16 [8192, 4096], P('seq', 'tp')
- filter_grad: float32 [4096, 128], P('tp')
The draws below stay inside these ranges and needn't reach their ends.
All inputs are finite; a program needn't handle non-finite values.
Results may differ from the reference program's by a relative error of at most 0.0018.
Values may be sent and summed in bfloat16 or wider, within the bound.
A program may use at most 128 MiB of HBM per device.

```python
import math
import jax
import jax.numpy as jnp
from jax import lax

C = 4096
K = 128
MODES = 16
TOKENS = 8192


def level_of(stream_key, shape, split, smallest, top_value):
    def one(dim, shards_of):
        heights = jax.random.uniform(jax.random.fold_in(jax.random.fold_in(stream_key, 6), dim), (shards_of,), jnp.float32, smallest / len(split), top_value / len(split))
        return jnp.repeat(jnp.exp(heights), shape[dim] // shards_of).reshape((-1,) + (1,) * (len(shape) - dim - 1))

    gain = one(*split[0])
    for cut in split[1:]:
        gain = gain * one(*cut)
    return gain


def normal_values(own_key, shape, width, bound, pieces=(), kind=jnp.bfloat16):
    result = jax.random.normal(own_key, shape, jnp.float32) * width
    if len(pieces) > 0:
        result = level_of(own_key, shape, pieces, -0.22, 0.18) * result
    return jnp.clip(result, min=-bound, max=bound).astype(kind)


def setup_inputs(seed: int = 0) -> dict:
    keys = jax.random.split(jax.random.key(seed), 8)
    q_gate = normal_values(keys[0], (TOKENS, C), 1.0, 6.0, ((0, 256),))
    key_in = normal_values(keys[1], (TOKENS, C), 1.0, 6.0, ((0, 256),))
    value_in = normal_values(keys[2], (TOKENS, C), 1.0, 6.0, ((0, 256),))
    out_grad = normal_values(keys[3], (TOKENS, C), 1.0, 6.0, ((0, 256),))
    mr_filter = normal_values(keys[4], (C, K), K ** -0.5, 0.5, ((0, 4),), jnp.float32)
    residues = normal_values(keys[5], (C, MODES), 0.25, 1.5, ((0, 4),), jnp.float32)
    decay_rates = jnp.clip(jnp.exp(math.log(0.05) - 9.010913 * jax.random.uniform(keys[6], (C, MODES), jnp.float32) ** level_of(keys[6], (C, MODES), ((0, 4),), -0.2, 0.2)), 6.10351571594947e-06, 0.05)
    return dict(q_gate=q_gate, key_in=key_in, value_in=value_in, out_grad=out_grad, mr_filter=mr_filter, residues=residues, decay_rates=decay_rates)


def tap_sum(signal, filters, backward):
    length = signal.shape[0] - filters.shape[1] + 1
    taps = filters.shape[1]

    def add_tap(index, total):
        tap = jnp.asarray(index).astype(jnp.int32)
        start = jnp.where(backward, tap, taps - 1 - tap).astype(jnp.int32)
        window = lax.dynamic_slice_in_dim(signal, start, length, 0)
        weight = lax.dynamic_slice_in_dim(filters, tap, 1, 1)[:, 0]
        return total + window * weight[None, :]
    initial = jnp.zeros((length, signal.shape[1]), signal.dtype)
    return lax.fori_loop(0, taps, add_tap, initial)

def reference(q_gate, key_in, value_in, out_grad, mr_filter, residues, decay_rates):
    query_rows = q_gate.astype(jnp.float32)
    key_rows = key_in.astype(jnp.float32)
    value_rows = value_in.astype(jnp.float32)
    upstream = out_grad.astype(jnp.float32)
    gated = key_rows * value_rows
    padded = jnp.pad(gated, ((K - 1, 0), (0, 0)))
    short_out = tap_sum(padded, mr_filter, False)
    decays = jnp.exp(-decay_rates)
    mode_gain = residues * jnp.sqrt(-jnp.expm1(-2.0 * decay_rates))

    def recur(carried, column):
        carried = decays * carried + column[:, None]
        return (carried, lax.optimization_barrier(jnp.sum(mode_gain * carried, axis=1)))
    initial = jnp.zeros(decay_rates.shape, jnp.float32)
    _, long_out = lax.scan(recur, initial, short_out)
    q_grad = (upstream * long_out).astype(jnp.bfloat16)
    gated_grad = query_rows * upstream
    _, short_grad = lax.scan(recur, initial, gated_grad, reverse=True)
    trailing = jnp.pad(short_grad, ((0, K - 1), (0, 0)))
    mixed_grad = tap_sum(trailing, mr_filter, True)
    key_grad = (mixed_grad * value_rows).astype(jnp.bfloat16)
    value_grad = (mixed_grad * key_rows).astype(jnp.bfloat16)
    length = short_grad.shape[0]

    def one_tap(tap):
        start = (K - 1 - tap).astype(jnp.int32)
        window = lax.dynamic_slice_in_dim(padded, start, length, 0)
        return lax.optimization_barrier(jnp.sum(short_grad * window, axis=0))
    columns = lax.map(one_tap, jnp.arange(K, dtype=jnp.int32))
    filter_grad = jnp.transpose(columns)
    return (q_grad, key_grad, value_grad, filter_grad)
```

```python
import functools

import jax
import jax.numpy as jnp
from jax import lax
from jax.experimental import pallas as pl
from jax.experimental.pallas import tpu as pltpu
from jax.sharding import PartitionSpec as P

MESH = pl.DeviceIdType.MESH
SEGS = 8
SPAN = 128
LANES = 128
TAPS = 128
MODES = 16
PLANE = SEGS * SPAN
TB, MB = 16, 8
STAGES = 14
KEY, VALUE, QUERY, UP, HALO_F, HALO_B, ST_F, ST_B, OUT_Q, OUT_K, OUT_V, RS, AG1, AG2 = range(STAGES)


def kernel(
    planes,
    parts,
    q_hbm,
    k_hbm,
    v_hbm,
    u_hbm,
    filt_hbm,
    res_hbm,
    dec_hbm,
    qg_out,
    kg_out,
    vg_out,
    fg_out,
    in_k,
    in_v,
    in_q,
    in_u,
    filt,
    res,
    dec,
    padded,
    taps_t,
    modes_t,
    tap,
    decay,
    gain,
    d128,
    d256,
    d512,
    lead_f,
    lead_b,
    gated_n,
    gated,
    short,
    grad_n,
    grad,
    excl_f,
    excl_b,
    total,
    states_f,
    states_b,
    enter,
    long_n,
    sg_n,
    sg,
    mixed_n,
    out_q,
    out_k,
    out_v,
    fsum,
    fpart,
    frecv,
    fmine,
    send,
    recv,
    local,
):
    rows = SPAN // parts
    chunks = SEGS * parts
    piece = TAPS // planes
    seq, p = lax.axis_index("seq"), lax.axis_index("tp")
    z, i = seq // SEGS, seq % SEGS
    here = i * parts + p

    def plane_peer(d):
        other = (here + d) % chunks
        return other, (z * SEGS + other // parts, other % parts)

    def row_peer(d):
        other = (i + d) % SEGS
        return other, (z * SEGS + other, p)

    def z_peer(d):
        other = (z + d) % planes
        return other, (other * SEGS + i, p)

    def push(stage, src, dst, device):
        pltpu.make_async_remote_copy(
            src_ref=src,
            dst_ref=dst,
            send_sem=send.at[stage],
            recv_sem=recv.at[stage],
            device_id=device,
            device_id_type=MESH,
        ).start()

    def keep(stage, src, dst):
        pltpu.make_async_copy(src, dst, recv.at[stage]).start()

    def await_bytes(sem, like):
        pltpu.make_async_copy(like, like, sem).wait()

    mine = pl.ds(pl.multiple_of(i * LANES, LANES), LANES)
    params = [
        pltpu.make_async_copy(filt_hbm.at[mine], filt, local.at[0]),
        pltpu.make_async_copy(res_hbm.at[mine], res, local.at[1]),
        pltpu.make_async_copy(dec_hbm.at[mine], dec, local.at[2]),
    ]
    for copy in params:
        copy.start()

    barrier = pltpu.get_barrier_semaphore()

    @pl.loop(1, chunks)
    def _(d):
        pl.semaphore_signal(barrier, inc=1, device_id=plane_peer(d)[1], device_id_type=MESH)

    @pl.loop(1, planes)
    def _(d):
        pl.semaphore_signal(barrier, inc=1, device_id=z_peer(d)[1], device_id_type=MESH)

    pl.semaphore_wait(barrier, chunks - 1 + planes - 1)

    def columns(chunk):
        segment, part = chunk // parts, chunk % parts
        start = part * PLANE + segment * LANES
        return pl.ds(pl.multiple_of(start, LANES), LANES)

    def scatter(pairs):
        @pl.loop(1, chunks)
        def _(d):
            other, device = plane_peer(d)
            for stage, src, dst in pairs:
                push(stage, src.at[:, columns(other)], dst.at[here], device)

        for stage, src, dst in pairs:
            keep(stage, src.at[:, columns(here)], dst.at[here])

    scatter([(KEY, k_hbm, in_k), (VALUE, v_hbm, in_v)])
    scatter([(QUERY, q_hbm, in_q), (UP, u_hbm, in_u)])

    for copy in params:
        copy.wait()
    taps_t[...] = jnp.transpose(filt[...])

    @pl.loop(0, TAPS)
    def _(m):
        tap[m] = jnp.broadcast_to(taps_t[pl.ds(m, 1), :], (SEGS, LANES))

    padded[...] = jnp.zeros_like(padded)
    padded[:, 0:MODES] = res[...]
    padded[:, MODES : 2 * MODES] = dec[...]
    modes_t[...] = jnp.transpose(padded[...])
    segment = lax.broadcasted_iota(jnp.int32, (SEGS, LANES), 0)
    seg_f = segment.astype(jnp.float32)

    @pl.loop(0, MODES)
    def _(n):
        rate = jnp.broadcast_to(modes_t[pl.ds(MODES + n, 1), :], (SEGS, LANES))
        weight = jnp.broadcast_to(modes_t[pl.ds(n, 1), :], (SEGS, LANES))
        u = 2.0 * rate
        series = jnp.ones_like(u)
        for order in range(8, 1, -1):
            series = 1.0 - (u * (1.0 / order)) * series
        decay[n] = jnp.exp(-rate)
        gain[n] = weight * jnp.sqrt(u * series)
        d128[n] = jnp.exp(-128.0 * rate)
        d256[n] = jnp.exp(-256.0 * rate)
        d512[n] = jnp.exp(-512.0 * rate)
        lead_f[n] = jnp.exp(-128.0 * rate * seg_f)
        lead_b[n] = jnp.exp(-128.0 * rate * (7.0 - seg_f))

    plane_decay = jnp.exp(-float(PLANE) * modes_t[MODES : 2 * MODES, :])

    def product(left, right, dst, offset):
        @pl.loop(0, chunks)
        def _(c):
            value = left[c].astype(jnp.float32) * right[c].astype(jnp.float32)
            dst[pl.ds(pl.multiple_of(offset + c * rows, rows), rows), :] = value

    await_bytes(recv.at[KEY], in_k)
    await_bytes(recv.at[VALUE], in_v)
    product(in_k, in_v, gated_n, SPAN)
    push(HALO_F, gated_n.at[pl.ds(PLANE, SPAN)], gated_n.at[pl.ds(0, SPAN)], z_peer(1)[1])

    @pl.loop(0, SPAN)
    def _(j):
        gated[SPAN + j] = gated_n[pl.ds(SPAN + j, SEGS, stride=SPAN), :]

    await_bytes(recv.at[HALO_F], gated_n.at[pl.ds(0, SPAN)])
    no_past = (segment == 0) & (z == 0)

    @pl.loop(0, SPAN)
    def _(j):
        gated[j] = jnp.where(no_past, 0.0, gated_n[pl.ds(j, SEGS, stride=SPAN), :])

    def blocks(count, inner, load, store):
        def body(b, carry):
            first = b * TB

            def step(s, acc):
                return load(first, s * MB, acc)

            acc = lax.fori_loop(
                0, inner, step, tuple(jnp.zeros((SEGS, LANES), jnp.float32) for _ in range(TB))
            )
            store(first, acc)
            return carry

        lax.fori_loop(0, count, body, 0)

    def fir_past(t, m, acc):
        window = gated[pl.ds(SPAN + t - m - (MB - 1), TB + MB - 1)]
        weights = tap[pl.ds(m, MB)]
        acc = list(acc)
        for b in range(MB):
            for a in range(TB):
                acc[a] = acc[a] + weights[b] * window[a - b + MB - 1]
        return tuple(acc)

    def fir_ahead(t, m, acc):
        window = sg[pl.ds(t + m, TB + MB - 1)]
        weights = tap[pl.ds(m, MB)]
        acc = list(acc)
        for b in range(MB):
            for a in range(TB):
                acc[a] = acc[a] + weights[b] * window[a + b]
        return tuple(acc)

    def correlate(m, t, acc):
        window = gated[pl.ds(SPAN + t - m - (TB - 1), TB + MB - 1)]
        ahead = sg[pl.ds(t, MB)]
        acc = list(acc)
        for b in range(MB):
            for a in range(TB):
                acc[a] = acc[a] + ahead[b] * window[b - a + TB - 1]
        return tuple(acc)

    def store_short(t, acc):
        for a in range(TB):
            short[t + a] = acc[a]

    def store_mixed(t, acc):
        for a in range(TB):
            mixed_n[pl.ds(t + a, SEGS, stride=SPAN), :] = acc[a]

    def store_fsum(m, acc):
        for a in range(TB):
            fsum[pl.ds(pl.multiple_of((m + a) * SEGS, SEGS), SEGS), :] = acc[a]

    blocks(SPAN // TB, TAPS // MB, fir_past, store_short)

    def end_state(source, backward):
        rates = [decay[n] for n in range(MODES)]

        def step(j, state):
            x = source[SPAN - 1 - j if backward else j]
            return tuple(rates[n] * state[n] + x for n in range(MODES))

        zero = jnp.zeros((SEGS, LANES), jnp.float32)
        return lax.fori_loop(0, SPAN, step, (zero,) * MODES, unroll=4)

    def shift(x, k, backward):
        if backward:
            return jnp.where(segment < SEGS - k, pltpu.roll(x, SEGS - k, 0), 0.0)
        return jnp.where(segment >= k, pltpu.roll(x, k, 0), 0.0)

    def share_states(state, excl, states, stage, backward):
        for n in range(MODES):
            x = state[n]
            x = x + d128[n] * shift(x, 1, backward)
            x = x + d256[n] * shift(x, 2, backward)
            x = x + d512[n] * shift(x, 4, backward)
            excl[n] = shift(x, 1, backward)
            edge = x[0:1, :] if backward else x[SEGS - 1 : SEGS, :]
            total[n : n + 1, :] = edge
        states[z] = total[...]

        @pl.loop(1, planes)
        def _(d):
            push(stage, states.at[z], states.at[z], z_peer(d)[1])

    def entering(excl, lead, states, stage, backward):
        await_bytes(recv.at[stage], states.at[pl.ds(0, planes - 1)])
        carried = jnp.zeros((MODES, LANES), jnp.float32)
        order = range(planes - 1, -1, -1) if backward else range(planes)
        for other in order:
            counts = (other > z) if backward else (other < z)
            carried = jnp.where(counts, plane_decay * carried + states[other], carried)
        enter[...] = carried
        return tuple(
            excl[n] + lead[n] * jnp.broadcast_to(enter[n : n + 1, :], (SEGS, LANES))
            for n in range(MODES)
        )

    def run(source, state, backward, emit):
        rates = [decay[n] for n in range(MODES)]

        def step(k, state):
            j = SPAN - 1 - k if backward else k
            x = source[j]
            state = tuple(rates[n] * state[n] + x for n in range(MODES))
            terms = [gain[n] * state[n] for n in range(MODES)]
            while len(terms) > 1:
                terms = [a + b for a, b in zip(terms[::2], terms[1::2])]
            emit(j, terms[0])
            return state

        lax.fori_loop(0, SPAN, step, state, unroll=2)

    share_states(end_state(short, False), excl_f, states_f, ST_F, False)

    await_bytes(recv.at[QUERY], in_q)
    await_bytes(recv.at[UP], in_u)
    product(in_q, in_u, grad_n, 0)

    @pl.loop(0, SPAN)
    def _(j):
        grad[j] = grad_n[pl.ds(j, SEGS, stride=SPAN), :]

    share_states(end_state(grad, True), excl_b, states_b, ST_B, True)

    def emit_long(j, y):
        long_n[pl.ds(j, SEGS, stride=SPAN), :] = y

    def emit_sg(j, y):
        sg_n[pl.ds(j, SEGS, stride=SPAN), :] = y
        sg[j] = y

    def output(stage, scaled_by, values, staged, out):
        @pl.loop(0, chunks)
        def _(c):
            value = values[pl.ds(pl.multiple_of(c * rows, rows), rows), :]
            value = value * scaled_by[c].astype(jnp.float32)
            staged[c] = value.astype(jnp.bfloat16)

        place = out.at[:, :, mine]

        @pl.loop(1, SEGS)
        def _(d):
            other, device = row_peer(d)
            push(stage, staged.at[pl.ds(other * parts, parts)], place, device)

        keep(stage, staged.at[pl.ds(i * parts, parts)], place)

    run(grad, entering(excl_b, lead_b, states_b, ST_B, True), True, emit_sg)
    push(HALO_B, sg_n.at[pl.ds(0, SPAN)], sg_n.at[pl.ds(PLANE, SPAN)], z_peer(planes - 1)[1])
    run(short, entering(excl_f, lead_f, states_f, ST_F, False), False, emit_long)
    output(OUT_Q, in_u, long_n, out_q, qg_out)

    blocks(TAPS // TB, SPAN // MB, correlate, store_fsum)

    @pl.loop(0, TAPS // SEGS)
    def _(b):
        start = b * SEGS * SEGS
        value = fsum[pl.ds(start, SEGS, stride=SEGS), :]
        for s in range(1, SEGS):
            value = value + fsum[pl.ds(start + s, SEGS, stride=SEGS), :]
        taps_t[pl.ds(pl.multiple_of(b * SEGS, SEGS), SEGS), :] = value

    fpart[...] = jnp.transpose(taps_t[...]).reshape(planes, piece, TAPS)
    frecv[z] = fpart[z]

    @pl.loop(1, planes)
    def _(d):
        other, device = z_peer(d)
        push(RS, fpart.at[other], frecv.at[z], device)

    await_bytes(recv.at[HALO_B], sg_n.at[pl.ds(PLANE, SPAN)])
    no_future = (segment == SEGS - 1) & (z == planes - 1)

    @pl.loop(0, SPAN)
    def _(j):
        sg[SPAN + j] = jnp.where(no_future, 0.0, sg_n[pl.ds(SPAN + j, SEGS, stride=SPAN), :])

    own = pl.ds(pl.multiple_of(z * piece, piece), piece)

    def gather_rows():
        await_bytes(recv.at[RS], frecv.at[pl.ds(0, planes - 1)])
        value = frecv[0]
        for other in range(1, planes):
            value = value + frecv[other]
        fmine[...] = value
        place = fg_out.at[i, own]

        @pl.loop(1, SEGS)
        def _(d):
            push(AG1, fmine, place, row_peer(d)[1])

        keep(AG1, fmine, place)

    def gather_planes():
        await_bytes(recv.at[AG1], fg_out.at[:, pl.ds(0, piece)])

        @pl.loop(1, planes)
        def _(d):
            push(AG2, fg_out.at[:, own], fg_out.at[:, own], z_peer(d)[1])

    def fir_mixed(first, count):
        def load(t, m, acc):
            return fir_ahead(t + first * TB, m, acc)

        def store(t, acc):
            store_mixed(t + first * TB, acc)

        blocks(count, TAPS // MB, load, store)

    fir_mixed(0, 4)
    gather_rows()
    fir_mixed(4, 4)
    gather_planes()
    output(OUT_K, in_v, mixed_n, out_k, kg_out)
    output(OUT_V, in_k, mixed_n, out_v, vg_out)

    for stage, out in ((OUT_Q, qg_out), (OUT_K, kg_out), (OUT_V, vg_out)):
        await_bytes(recv.at[stage], out)
    await_bytes(recv.at[AG2], fg_out.at[:, pl.ds(0, (planes - 1) * piece)])
    for stage, like in (
        (KEY, in_k.at[pl.ds(0, chunks - 1)]),
        (VALUE, in_v.at[pl.ds(0, chunks - 1)]),
        (QUERY, in_q.at[pl.ds(0, chunks - 1)]),
        (UP, in_u.at[pl.ds(0, chunks - 1)]),
        (HALO_F, gated_n.at[pl.ds(0, SPAN)]),
        (HALO_B, sg_n.at[pl.ds(0, SPAN)]),
        (ST_F, states_f.at[pl.ds(0, planes - 1)]),
        (ST_B, states_b.at[pl.ds(0, planes - 1)]),
        (OUT_Q, out_q.at[pl.ds(0, chunks - parts)]),
        (OUT_K, out_k.at[pl.ds(0, chunks - parts)]),
        (OUT_V, out_v.at[pl.ds(0, chunks - parts)]),
        (RS, frecv.at[pl.ds(0, planes - 1)]),
        (AG1, fg_out.at[pl.ds(0, SEGS - 1), pl.ds(0, piece)]),
        (AG2, fg_out.at[:, pl.ds(0, (planes - 1) * piece)]),
    ):
        await_bytes(send.at[stage], like)


def body(planes, parts, q_gate, key_in, value_in, out_grad, mr_filter, residues, decay_rates):
    rows = SPAN // parts
    chunks = SEGS * parts
    piece = TAPS // planes
    f32, bf16 = jnp.float32, jnp.bfloat16

    def vmem(*shape, kind=f32):
        return pltpu.VMEM(shape, kind)

    arrived = vmem(chunks, rows, LANES, kind=bf16)
    per_mode = vmem(MODES, SEGS, LANES)
    scratch = [
        arrived,
        arrived,
        arrived,
        arrived,
        vmem(LANES, TAPS),
        vmem(LANES, MODES),
        vmem(LANES, MODES),
        vmem(LANES, LANES),
        vmem(TAPS, LANES),
        vmem(LANES, LANES),
        vmem(TAPS, SEGS, LANES),
        per_mode,
        per_mode,
        per_mode,
        per_mode,
        per_mode,
        per_mode,
        per_mode,
        vmem(PLANE + SPAN, LANES),
        vmem(2 * SPAN, SEGS, LANES),
        vmem(SPAN, SEGS, LANES),
        vmem(PLANE, LANES),
        vmem(SPAN, SEGS, LANES),
        per_mode,
        per_mode,
        vmem(MODES, LANES),
        vmem(planes, MODES, LANES),
        vmem(planes, MODES, LANES),
        vmem(MODES, LANES),
        vmem(PLANE, LANES),
        vmem(PLANE + SPAN, LANES),
        vmem(2 * SPAN, SEGS, LANES),
        vmem(PLANE, LANES),
        arrived,
        arrived,
        arrived,
        vmem(TAPS * SEGS, LANES),
        vmem(planes, piece, TAPS),
        vmem(planes, piece, TAPS),
        vmem(piece, TAPS),
        pltpu.SemaphoreType.DMA((STAGES,)),
        pltpu.SemaphoreType.DMA((STAGES,)),
        pltpu.SemaphoreType.DMA((3,)),
    ]
    hbm = pl.BlockSpec(memory_space=pl.ANY)
    out = jax.ShapeDtypeStruct((parts, rows, SEGS * LANES), bf16)
    results = pl.pallas_call(
        functools.partial(kernel, planes, parts),
        out_shape=(out, out, out, jax.ShapeDtypeStruct((SEGS, LANES, TAPS), f32)),
        in_specs=[hbm] * 7,
        out_specs=(hbm,) * 4,
        scratch_shapes=scratch,
        compiler_params=pltpu.CompilerParams(
            collective_id=0, has_side_effects=True, vmem_limit_bytes=40 * 1024 * 1024
        ),
    )(q_gate, key_in, value_in, out_grad, mr_filter, residues, decay_rates)
    grads = [part.reshape(SPAN, SEGS * LANES) for part in results[:3]]
    return (*grads, results[3].reshape(SEGS * LANES, TAPS))


def solution(mesh):
    rows = P(("seq", "tp"), None)
    return jax.shard_map(
        functools.partial(body, mesh.shape["seq"] // SEGS, mesh.shape["tp"]),
        mesh=mesh,
        in_specs=(rows, rows, rows, rows, P("tp", None), P("tp", None), P("tp", None)),
        out_specs=(P("seq", "tp"), P("seq", "tp"), P("seq", "tp"), P("tp", None)),
        check_vma=False,
    )
```

```python
import functools

import jax
import jax.numpy as jnp
from jax import lax
from jax.experimental import pallas as pl
from jax.experimental.pallas import tpu as pltpu
from jax.sharding import PartitionSpec as P

MESH = pl.DeviceIdType.MESH
SEGS = 8
SPAN = 128
LANES = 128
TAPS = 128
MODES = 16
PLANE = SEGS * SPAN
HALF = SPAN // 2
SUB = 32
PARTS = 9
TB, MB = 16, 16
VMEM = 40 * 1024 * 1024
(KV, QU, HALO_F, HALO_B, ST_F, ST_B, OUT_Q, OUT_K0, OUT_V0, OUT_K1, OUT_V1, RS, Z1, P1, Z2, P2) = range(16)
STAGES = 16


def kernel(
    planes,
    parts,
    q_hbm,
    k_hbm,
    v_hbm,
    u_hbm,
    filt_hbm,
    res_hbm,
    dec_hbm,
    qg_out,
    kg_out,
    vg_out,
    fg_out,
    stack,
    in_kv,
    in_qu,
    filt,
    res,
    dec,
    taps_t,
    tap,
    decay,
    gain,
    gated_n,
    gated_s,
    short,
    grad_n,
    ends_f,
    ends_b,
    starts,
    states_f,
    states_b,
    long_n,
    sg_n,
    sg_s,
    sg_w,
    prods,
    mixed_n,
    out_q,
    out_k,
    out_v,
    fsum,
    fpart,
    frecv,
    fmine,
    send,
    recv,
    local,
):
    rows = SPAN // parts
    chunks = SEGS * parts
    piece = TAPS // planes
    half_piece = piece // 2
    seq, p = lax.axis_index("seq"), lax.axis_index("tp")
    z, i = seq // SEGS, seq % SEGS
    here = i * parts + p

    def plane_peer(d):
        other = lax.rem(here + d, chunks)
        segment, part = lax.div(other, parts), lax.rem(other, parts)
        return segment, part, (z * SEGS + segment, part)

    def row_peer(d):
        other = lax.rem(i + d, SEGS)
        return other, (z * SEGS + other, p)

    def z_peer(d):
        other = lax.rem(z + d, planes)
        return other, (other * SEGS + i, p)

    def push(stage, src, dst, device):
        pltpu.make_async_remote_copy(
            src_ref=src,
            dst_ref=dst,
            send_sem=send.at[stage],
            recv_sem=recv.at[stage],
            device_id=device,
            device_id_type=MESH,
        ).start()

    def keep(stage, src, dst):
        pltpu.make_async_copy(src, dst, recv.at[stage]).start()

    def await_bytes(sem, like):
        pltpu.make_async_copy(like, like, sem).wait()

    barrier = pltpu.get_barrier_semaphore()

    @pl.loop(1, chunks)
    def _(d):
        pl.semaphore_signal(barrier, inc=1, device_id=plane_peer(d)[2], device_id_type=MESH)

    @pl.loop(1, planes)
    def _(d):
        pl.semaphore_signal(barrier, inc=1, device_id=z_peer(d)[1], device_id_type=MESH)

    mine = pl.ds(pl.multiple_of(i * LANES, LANES), LANES)
    loads = [
        pltpu.make_async_copy(src, stack.at[n], local.at[n])
        for n, src in enumerate((k_hbm, v_hbm, q_hbm, u_hbm))
    ]
    params = [
        pltpu.make_async_copy(filt_hbm.at[mine], filt, local.at[4]),
        pltpu.make_async_copy(res_hbm.at[:, mine], res, local.at[5]),
        pltpu.make_async_copy(dec_hbm.at[:, mine], dec, local.at[6]),
    ]
    for copy in loads + params:
        copy.start()
    for copy in loads:
        copy.wait()
    pl.semaphore_wait(barrier, chunks - 1 + planes - 1)

    def columns(segment, part):
        return pl.ds(pl.multiple_of(part * PLANE + segment * LANES, LANES), LANES)

    own_rows = pl.ds(pl.multiple_of(p * rows, rows), rows)

    def scatter(stage, first, dst):
        @pl.loop(1, chunks)
        def _(d):
            segment, part, device = plane_peer(d)
            src = stack.at[pl.ds(first, 2), :, columns(segment, part)]
            push(stage, src, dst.at[:, i, own_rows], device)

        keep(stage, stack.at[pl.ds(first, 2), :, columns(i, p)], dst.at[:, i, own_rows])

    scatter(KV, 0, in_kv)
    scatter(QU, 2, in_qu)

    for copy in params:
        copy.wait()
    taps_t[...] = jnp.transpose(filt[...])

    def combine_halves(quarters, swapped):
        a, b, c, d = quarters
        low, both, high = (a, b), (a + c, b + d), (c, d)
        result = []
        for first, second in (high, both, low) if swapped else (low, both, high):
            ends = (second, first + second, first) if swapped else (first, first + second, second)
            result += ends
        return result

    @pl.loop(0, SUB)
    def _(m):
        quarters = [
            jnp.broadcast_to(taps_t[pl.ds(m + SUB * s, 1), :], (SEGS, LANES)) for s in range(4)
        ]
        for g, value in enumerate(combine_halves(quarters, True)):
            tap[g, m] = value

    @pl.loop(0, MODES)
    def _(n):
        rate = jnp.broadcast_to(dec[pl.ds(n, 1), :], (SEGS, LANES))
        weight = jnp.broadcast_to(res[pl.ds(n, 1), :], (SEGS, LANES))
        u = 2.0 * rate
        series = jnp.ones_like(u)
        for order in range(8, 1, -1):
            series = 1.0 - (u * (1.0 / order)) * series
        decay[n] = jnp.exp(-rate)
        gain[n] = weight * jnp.sqrt(u * series)

    span_decay = jnp.exp(-float(SPAN) * dec[...])
    plane_decay = jnp.exp(-float(PLANE) * dec[...])

    def product(pair, dst, offset):
        @pl.loop(0, SEGS)
        def _(s):
            value = pair[0, s].astype(jnp.float32) * pair[1, s].astype(jnp.float32)
            dst[pl.ds(pl.multiple_of(offset + s * SPAN, SPAN), SPAN), :] = value

    def at_token(ref, j):
        return ref[pl.ds(j, SEGS, stride=SPAN), :]

    def differences(source, first, dst):
        @pl.loop(0, 2 * SUB - 1)
        def _(k):
            a = [at_token(source, first + k + SUB * s) for s in range(7)]
            before = [a[s] - a[s + 2] for s in range(3)]
            after = [a[s + 4] - a[s + 2] for s in range(3)]
            for u, (x, y, w) in enumerate((before, a[2:5], after)):
                dst[3 * u, k] = x - y
                dst[3 * u + 1, k] = y
                dst[3 * u + 2, k] = w - y

    def products(gen, vec, first, last, place, base, swapped):
        @pl.loop(first * 2, last * 2)
        def _(b):
            g, t = lax.div(b, 2), lax.rem(b, 2) * TB
            v = 8 - g if swapped else g
            acc = [jnp.zeros((SEGS, LANES), jnp.float32) for _ in range(TB)]
            for m0 in range(0, SUB, MB):
                low = min(place(0, m0), place(TB - 1, m0), place(0, m0 + MB - 1))
                window = gen[g, pl.ds(base(t) + low, TB + MB - 1)]
                weights = vec[v, pl.ds(m0, MB)]
                for m in range(MB):
                    for a in range(TB):
                        acc[a] = acc[a] + weights[m] * window[place(a, m0 + m) - low]
            for a in range(TB):
                prods[g, t + a] = acc[a]

    def recombine(store, halves, swapped):
        @pl.loop(0, SUB)
        def _(t):
            for top in halves:
                u = 3 * (2 - 2 * top if swapped else 2 * top)
                for low in range(2):
                    v = 2 - 2 * low if swapped else 2 * low
                    value = (prods[4, t] + prods[3 + v, t]) + (prods[u + 1, t] + prods[u + v, t])
                    store(top * HALF + low * SUB + t, value)

    def past_products(first, last):
        products(gated_s, tap, first, last, lambda a, m: SUB - 1 + a - m, lambda t: t, False)

    def ahead_products(first, last):
        products(sg_s, tap, first, last, lambda a, m: a + m, lambda t: t, True)

    def lag_products():
        products(gated_s, sg_w, 0, PARTS, lambda a, j: TB - 1 + j - a, lambda t: TB - t, False)

    def store_short(t, value):
        short[t] = value

    def store_mixed(t, value):
        mixed_n[pl.ds(t, SEGS, stride=SPAN), :] = value

    def store_fsum(m, value):
        fsum[pl.ds(pl.multiple_of(m * SEGS, SEGS), SEGS), :] = value

    def end_state(token, backward):
        rates = [decay[n] for n in range(MODES)]

        def step(j, state):
            x = token(SPAN - 1 - j if backward else j)
            return tuple(rates[n] * state[n] + x for n in range(MODES))

        zero = jnp.zeros((SEGS, LANES), jnp.float32)
        return lax.fori_loop(0, SPAN, step, (zero,) * MODES, unroll=4)

    def segments(backward):
        return range(SEGS - 1, -1, -1) if backward else range(SEGS)

    def share_states(state, ends, states, stage, backward):
        for n in range(MODES):
            ends[n * SEGS : (n + 1) * SEGS, :] = state[n]
        carried = jnp.zeros((MODES, LANES), jnp.float32)
        for s in segments(backward):
            carried = span_decay * carried + ends[pl.ds(s, MODES, stride=SEGS), :]
        states[z] = carried

        @pl.loop(1, planes)
        def _(d):
            push(stage, states.at[z], states.at[z], z_peer(d)[1])

    def entering(ends, states, stage, backward):
        await_bytes(recv.at[stage], states.at[pl.ds(0, planes - 1)])
        carried = jnp.zeros((MODES, LANES), jnp.float32)
        for other in range(planes - 1, -1, -1) if backward else range(planes):
            counts = (other > z) if backward else (other < z)
            carried = jnp.where(counts, plane_decay * carried + states[other], carried)
        for s in segments(backward):
            starts[pl.ds(s, MODES, stride=SEGS), :] = carried
            carried = span_decay * carried + ends[pl.ds(s, MODES, stride=SEGS), :]
        return tuple(starts[n * SEGS : (n + 1) * SEGS, :] for n in range(MODES))

    def run(token, state, backward, emit):
        rates = [decay[n] for n in range(MODES)]

        def step(k, state):
            j = SPAN - 1 - k if backward else k
            x = token(j)
            state = tuple(rates[n] * state[n] + x for n in range(MODES))
            terms = [gain[n] * state[n] for n in range(MODES)]
            while len(terms) > 1:
                terms = [a + b for a, b in zip(terms[::2], terms[1::2])]
            emit[pl.ds(j, SEGS, stride=SPAN), :] = terms[0]
            return state

        lax.fori_loop(0, SPAN, step, state, unroll=2)

    def output(stage, scaled_by, values, staged, out, first, count):
        @pl.loop(0, SEGS)
        def _(s):
            start = pl.multiple_of(s * SPAN + first, HALF)
            value = values[pl.ds(start, count), :] * scaled_by[s, pl.ds(first, count)].astype(jnp.float32)
            staged[s, pl.ds(first, count)] = value.astype(jnp.bfloat16)

        place = out.at[pl.ds(first, count), mine]

        @pl.loop(1, SEGS)
        def _(d):
            other, device = row_peer(d)
            push(stage, staged.at[other, pl.ds(first, count)], place, device)

        keep(stage, staged.at[i, pl.ds(first, count)], place)

    await_bytes(recv.at[KV], in_kv)
    product(in_kv, gated_n, SPAN)
    push(HALO_F, gated_n.at[pl.ds(PLANE, SPAN)], gated_n.at[pl.ds(0, SPAN)], z_peer(1)[1])
    await_bytes(recv.at[HALO_F], gated_n.at[pl.ds(0, SPAN)])

    @pl.when(z == 0)
    def _():
        gated_n[0:SPAN, :] = jnp.zeros((SPAN, LANES), jnp.float32)

    differences(gated_n, 1, gated_s)
    past_products(0, 6)

    await_bytes(recv.at[QU], in_qu)
    product(in_qu, grad_n, 0)

    def grad_token(j):
        return at_token(grad_n, j)

    share_states(end_state(grad_token, True), ends_b, states_b, ST_B, True)

    past_products(6, PARTS)
    recombine(store_short, (0, 1), False)

    def short_token(j):
        return short[j]

    share_states(end_state(short_token, False), ends_f, states_f, ST_F, False)

    run(grad_token, entering(ends_b, states_b, ST_B, True), True, sg_n)
    push(HALO_B, sg_n.at[pl.ds(0, SPAN)], sg_n.at[pl.ds(PLANE, SPAN)], z_peer(planes - 1)[1])

    @pl.loop(0, SUB)
    def _(j):
        quarters = [at_token(sg_n, j + SUB * s) for s in range(4)]
        for g, value in enumerate(combine_halves(quarters, False)):
            sg_w[g, j] = value

    lag_products()
    recombine(store_fsum, (0, 1), True)

    @pl.loop(0, TAPS // SEGS)
    def _(b):
        start = b * SEGS * SEGS
        value = fsum[pl.ds(start, SEGS, stride=SEGS), :]
        for s in range(1, SEGS):
            value = value + fsum[pl.ds(start + s, SEGS, stride=SEGS), :]
        taps_t[pl.ds(pl.multiple_of(b * SEGS, SEGS), SEGS), :] = value

    fpart[...] = jnp.transpose(taps_t[...]).reshape(planes, piece, TAPS)
    frecv[z] = fpart[z]

    @pl.loop(1, planes)
    def _(d):
        other, device = z_peer(d)
        push(RS, fpart.at[other], frecv.at[z], device)

    run(short_token, entering(ends_f, states_f, ST_F, False), False, long_n)
    output(OUT_Q, in_qu.at[1], long_n, out_q, qg_out, 0, SPAN)

    over_z, over_plane = pl.ds(0, half_piece), pl.ds(half_piece, half_piece)

    def sum_planes():
        await_bytes(recv.at[RS], frecv.at[pl.ds(0, planes - 1)])
        value = frecv[0]
        for other in range(1, planes):
            value = value + frecv[other]
        fmine[...] = value
        z_place, plane_place = fg_out.at[i, z, over_z], fg_out.at[i, z, over_plane]

        @pl.loop(1, planes)
        def _(d):
            push(Z1, fmine.at[over_z], z_place, z_peer(d)[1])

        @pl.loop(1, SEGS)
        def _(d):
            push(P1, fmine.at[over_plane], plane_place, row_peer(d)[1])

        keep(Z1, fmine.at[over_z], z_place)
        keep(P1, fmine.at[over_plane], plane_place)

    def spread():
        await_bytes(recv.at[P1], fg_out.at[:, 0, over_plane])

        @pl.loop(1, planes)
        def _(d):
            place = fg_out.at[:, z, over_plane]
            push(P2, place, place, z_peer(d)[1])

        await_bytes(recv.at[Z1], fg_out.at[0, :, over_z])

        @pl.loop(1, SEGS)
        def _(d):
            place = fg_out.at[i, :, over_z]
            push(Z2, place, place, row_peer(d)[1])

    await_bytes(recv.at[HALO_B], sg_n.at[pl.ds(PLANE, SPAN)])

    @pl.when(z == planes - 1)
    def _():
        sg_n[PLANE : PLANE + SPAN, :] = jnp.zeros((SPAN, LANES), jnp.float32)

    differences(sg_n, 0, sg_s)
    sum_planes()
    ahead_products(0, 6)
    recombine(store_mixed, (0,), False)
    output(OUT_K0, in_kv.at[1], mixed_n, out_k, kg_out, 0, HALF)
    output(OUT_V0, in_kv.at[0], mixed_n, out_v, vg_out, 0, HALF)
    spread()
    ahead_products(6, PARTS)
    recombine(store_mixed, (1,), False)
    output(OUT_K1, in_kv.at[1], mixed_n, out_k, kg_out, HALF, HALF)
    output(OUT_V1, in_kv.at[0], mixed_n, out_v, vg_out, HALF, HALF)

    low, high = pl.ds(0, HALF), pl.ds(HALF, HALF)
    others = pl.ds(0, SEGS - 1)
    other_planes = pl.ds(0, planes - 1)
    for stage, like in (
        (OUT_Q, qg_out),
        (OUT_K0, kg_out.at[low]),
        (OUT_V0, vg_out.at[low]),
        (Z2, fg_out.at[others, :, over_z]),
        (P2, fg_out.at[:, other_planes, over_plane]),
        (OUT_K1, kg_out.at[high]),
        (OUT_V1, vg_out.at[high]),
    ):
        await_bytes(recv.at[stage], like)
    most = pl.ds(0, SEGS - 1)
    for stage, like in (
        (HALO_F, gated_n.at[pl.ds(0, SPAN)]),
        (HALO_B, sg_n.at[pl.ds(0, SPAN)]),
        (ST_F, states_f.at[other_planes]),
        (ST_B, states_b.at[other_planes]),
        (OUT_Q, out_q.at[most]),
        (OUT_K0, out_k.at[most, low]),
        (OUT_V0, out_v.at[most, low]),
        (OUT_K1, out_k.at[most, high]),
        (OUT_V1, out_v.at[most, high]),
        (RS, frecv.at[other_planes]),
        (Z1, fg_out.at[0, other_planes, over_z]),
        (P1, fg_out.at[others, 0, over_plane]),
        (Z2, fg_out.at[others, :, over_z]),
        (P2, fg_out.at[:, other_planes, over_plane]),
    ):
        await_bytes(send.at[stage], like)
    for stage, like in ((KV, in_kv), (QU, in_qu)):
        await_bytes(send.at[stage], like.at[:, pl.ds(0, SEGS - 1)])
        if parts > 1:
            await_bytes(send.at[stage], like.at[:, 0, pl.ds(0, SPAN - rows)])


def finish(*refs):
    sources, results, done = refs[:4], refs[4:8], refs[8]
    copies = [
        pltpu.make_async_copy(src, dst, done.at[n])
        for n, (src, dst) in enumerate(zip(sources, results))
    ]
    for copy in copies:
        copy.start()
    for copy in copies:
        copy.wait()


def body(planes, parts, q_gate, key_in, value_in, out_grad, mr_filter, residues, decay_rates):
    piece = TAPS // planes
    f32, bf16 = jnp.float32, jnp.bfloat16

    def vmem(*shape, kind=f32):
        return pltpu.VMEM(shape, kind)

    scratch = [
        vmem(4, *q_gate.shape, kind=bf16),
        vmem(2, SEGS, SPAN, LANES, kind=bf16),
        vmem(2, SEGS, SPAN, LANES, kind=bf16),
        vmem(LANES, TAPS),
        vmem(MODES, LANES),
        vmem(MODES, LANES),
        vmem(TAPS, LANES),
        vmem(PARTS, SUB, SEGS, LANES),
        vmem(MODES, SEGS, LANES),
        vmem(MODES, SEGS, LANES),
        vmem(PLANE + SPAN, LANES),
        vmem(PARTS, 2 * SUB, SEGS, LANES),
        vmem(SPAN, SEGS, LANES),
        vmem(PLANE, LANES),
        vmem(MODES * SEGS, LANES),
        vmem(MODES * SEGS, LANES),
        vmem(MODES * SEGS, LANES),
        vmem(planes, MODES, LANES),
        vmem(planes, MODES, LANES),
        vmem(PLANE, LANES),
        vmem(PLANE + SPAN, LANES),
        vmem(PARTS, 2 * SUB, SEGS, LANES),
        vmem(PARTS, SUB, SEGS, LANES),
        vmem(PARTS, SUB, SEGS, LANES),
        vmem(PLANE, LANES),
        vmem(SEGS, SPAN, LANES, kind=bf16),
        vmem(SEGS, SPAN, LANES, kind=bf16),
        vmem(SEGS, SPAN, LANES, kind=bf16),
        vmem(TAPS * SEGS, LANES),
        vmem(planes, piece, TAPS),
        vmem(planes, piece, TAPS),
        vmem(piece, TAPS),
        pltpu.SemaphoreType.DMA((STAGES,)),
        pltpu.SemaphoreType.DMA((STAGES,)),
        pltpu.SemaphoreType.DMA((7,)),
    ]
    anywhere = pl.BlockSpec(memory_space=pl.ANY)
    hbm = pl.BlockSpec(memory_space=pltpu.HBM)
    out = jax.ShapeDtypeStruct((SPAN, SEGS * LANES), bf16)
    shapes = (out, out, out, jax.ShapeDtypeStruct((SEGS, planes, piece, TAPS), f32))
    operands = (q_gate, key_in, value_in, out_grad, mr_filter, residues.T, decay_rates.T)
    operands = [pltpu.with_memory_space_constraint(x, pltpu.HBM) for x in operands]
    results = pl.pallas_call(
        functools.partial(kernel, planes, parts),
        out_shape=tuple(pltpu.VMEM(x.shape, x.dtype) for x in shapes),
        in_specs=[hbm] * 7,
        out_specs=(anywhere,) * 4,
        scratch_shapes=scratch,
        compiler_params=pltpu.CompilerParams(
            collective_id=0, has_side_effects=True, vmem_limit_bytes=VMEM
        ),
    )(*operands)
    *grads, filter_grad = pl.pallas_call(
        finish,
        out_shape=tuple(pltpu.HBM(x.shape, x.dtype) for x in shapes),
        in_specs=[anywhere] * 4,
        out_specs=(hbm,) * 4,
        scratch_shapes=[pltpu.SemaphoreType.DMA((4,))],
        compiler_params=pltpu.CompilerParams(vmem_limit_bytes=VMEM),
    )(*results)
    return (*grads, filter_grad.reshape(SEGS * LANES, TAPS))


def solution(mesh):
    rows = P(("seq", "tp"), None)
    return jax.shard_map(
        functools.partial(body, mesh.shape["seq"] // SEGS, mesh.shape["tp"]),
        mesh=mesh,
        in_specs=(rows, rows, rows, rows, P("tp", None), P("tp", None), P("tp", None)),
        out_specs=(P("seq", "tp"), P("seq", "tp"), P("seq", "tp"), P("tp", None)),
        check_vma=False,
    )
```

```python
import functools

import jax
import jax.numpy as jnp
from jax import lax
from jax.experimental import pallas as pl
from jax.experimental.pallas import tpu as pltpu
from jax.sharding import PartitionSpec as P

MESH = pl.DeviceIdType.MESH
SEGS = 8
SPAN = 128
LANES = 128
TAPS = 128
MODES = 16
PLANE = SEGS * SPAN
HALF = SPAN // 2
SUB = 32
PARTS = 9
TB, MB = 16, 16
VMEM = 40 * 1024 * 1024
(KV, QU, HALO_F, HALO_B, HALO_U, ST_F, ST_B, OUT_Q0, OUT_Q1, OUT_K0, OUT_V0, OUT_K1, OUT_V1, RS, Z1, P1, Z2, P2) = range(18)
STAGES = 18
PITCH = SPAN + 8


def kernel(
    planes,
    parts,
    q_hbm,
    k_hbm,
    v_hbm,
    u_hbm,
    filt_hbm,
    res_hbm,
    dec_hbm,
    qg_out,
    kg_out,
    vg_out,
    fg_out,
    stack,
    in_kv,
    in_qu,
    filt,
    res,
    dec,
    taps_t,
    tap,
    decay,
    gain,
    gated_n,
    gated,
    gated_s,
    u,
    grad_n,
    grad,
    ends_f,
    ends_b,
    starts,
    states_f,
    states_b,
    long_n,
    sg,
    sg_s,
    sg_w,
    past,
    first_sg,
    future,
    last_u,
    past_u,
    prods,
    mixed_n,
    out_q,
    out_k,
    out_v,
    fsum,
    fpart,
    frecv,
    fmine,
    send,
    recv,
    local,
):
    rows = SPAN // parts
    chunks = SEGS * parts
    piece = TAPS // planes
    half_piece = piece // 2
    seq, p = lax.axis_index("seq"), lax.axis_index("tp")
    z, i = seq // SEGS, seq % SEGS
    here = i * parts + p

    def plane_peer(d):
        other = lax.rem(here + 5 * d, chunks)
        segment, part = lax.div(other, parts), lax.rem(other, parts)
        return segment, part, (z * SEGS + segment, part)

    def row_peer(d):
        other = lax.rem(i + d, SEGS)
        return other, (z * SEGS + other, p)

    def z_peer(d):
        other = lax.rem(z + d, planes)
        return other, (other * SEGS + i, p)

    def push(stage, src, dst, device):
        pltpu.make_async_remote_copy(
            src_ref=src,
            dst_ref=dst,
            send_sem=send.at[stage],
            recv_sem=recv.at[stage],
            device_id=device,
            device_id_type=MESH,
        ).start()

    def keep(stage, src, dst):
        pltpu.make_async_copy(src, dst, recv.at[stage]).start()

    def await_bytes(sem, like):
        pltpu.make_async_copy(like, like, sem).wait()

    barrier = pltpu.get_barrier_semaphore()

    @pl.loop(1, chunks)
    def _(d):
        pl.semaphore_signal(barrier, inc=1, device_id=plane_peer(d)[2], device_id_type=MESH)

    @pl.loop(1, planes)
    def _(d):
        pl.semaphore_signal(barrier, inc=1, device_id=z_peer(d)[1], device_id_type=MESH)

    mine = pl.ds(pl.multiple_of(i * LANES, LANES), LANES)
    loads = [
        pltpu.make_async_copy(src, stack.at[n], local.at[n])
        for n, src in enumerate((k_hbm, v_hbm, q_hbm, u_hbm))
    ]
    params = [
        pltpu.make_async_copy(filt_hbm.at[mine], filt, local.at[4]),
        pltpu.make_async_copy(res_hbm.at[:, mine], res, local.at[5]),
        pltpu.make_async_copy(dec_hbm.at[:, mine], dec, local.at[6]),
    ]
    for copy in loads + params:
        copy.start()
    for copy in loads:
        copy.wait()
    pl.semaphore_wait(barrier, chunks - 1 + planes - 1)

    def columns(segment, part):
        return pl.ds(pl.multiple_of(part * PLANE + segment * LANES, LANES), LANES)

    own_rows = pl.ds(pl.multiple_of(p * rows, rows), rows)

    def scatter(stage, first, dst):
        @pl.loop(1, chunks)
        def _(d):
            segment, part, device = plane_peer(d)
            src = stack.at[pl.ds(first, 2), :, columns(segment, part)]
            push(stage, src, dst.at[:, i, own_rows], device)

        keep(stage, stack.at[pl.ds(first, 2), :, columns(i, p)], dst.at[:, i, own_rows])

    scatter(QU, 2, in_qu)
    scatter(KV, 0, in_kv)

    for copy in params:
        copy.wait()
    taps_t[...] = jnp.transpose(filt[...])

    def combine_halves(quarters, swapped):
        a, b, c, d = quarters
        low, both, high = (a, b), (a + c, b + d), (c, d)
        result = []
        for first, second in (high, both, low) if swapped else (low, both, high):
            ends = (second, first + second, first) if swapped else (first, first + second, second)
            result += ends
        return result

    @pl.loop(0, SUB)
    def _(m):
        quarters = [
            jnp.broadcast_to(taps_t[pl.ds(m + SUB * s, 1), :], (SEGS, LANES)) for s in range(4)
        ]
        for g, value in enumerate(combine_halves(quarters, True)):
            tap[g, m] = value

    @pl.loop(0, MODES)
    def _(n):
        rate = jnp.broadcast_to(dec[pl.ds(n, 1), :], (SEGS, LANES))
        weight = jnp.broadcast_to(res[pl.ds(n, 1), :], (SEGS, LANES))
        u = 2.0 * rate
        series = jnp.ones_like(u)
        for order in range(8, 1, -1):
            series = 1.0 - (u * (1.0 / order)) * series
        decay[n] = jnp.exp(-rate)
        gain[n] = weight * jnp.sqrt(u * series)

    span_decay = jnp.exp(-float(SPAN) * dec[...])
    plane_decay = jnp.exp(-float(PLANE) * dec[...])

    segment = lax.broadcasted_iota(jnp.int32, (SEGS, LANES), 0)

    def product(pair, dst):
        @pl.loop(0, SEGS)
        def _(s):
            value = pair[0, s].astype(jnp.float32) * pair[1, s].astype(jnp.float32)
            dst[pl.ds(pl.multiple_of(s * PITCH, 8), SPAN), :] = value

    def by_segment(source, dst, first):
        @pl.loop(0, SPAN, unroll=4)
        def _(j):
            dst[first + j] = source[pl.ds(j, SEGS, stride=PITCH), :]

    def differences(source, first, dst):
        @pl.loop(0, 2 * SUB - 1)
        def _(k):
            a = [source[first + k + SUB * s] for s in range(7)]
            before = [a[s] - a[s + 2] for s in range(3)]
            after = [a[s + 4] - a[s + 2] for s in range(3)]
            for u, (x, y, w) in enumerate((before, a[2:5], after)):
                dst[3 * u, k] = x - y
                dst[3 * u + 1, k] = y
                dst[3 * u + 2, k] = w - y

    def products(gen, vec, first, last, place, base, swapped):
        @pl.loop(first * 2, last * 2)
        def _(b):
            g, t = lax.div(b, 2), lax.rem(b, 2) * TB
            v = 8 - g if swapped else g
            acc = [jnp.zeros((SEGS, LANES), jnp.float32) for _ in range(TB)]
            for m0 in range(0, SUB, MB):
                low = min(place(0, m0), place(TB - 1, m0), place(0, m0 + MB - 1))
                window = gen[g, pl.ds(base(t) + low, TB + MB - 1)]
                weights = vec[v, pl.ds(m0, MB)]
                for m in range(MB):
                    for a in range(TB):
                        acc[a] = acc[a] + weights[m] * window[place(a, m0 + m) - low]
            for a in range(TB):
                prods[g, t + a] = acc[a]

    def recombine(store, halves, swapped):
        @pl.loop(0, SUB)
        def _(t):
            for top in halves:
                u = 3 * (2 - 2 * top if swapped else 2 * top)
                for low in range(2):
                    v = 2 - 2 * low if swapped else 2 * low
                    value = (prods[4, t] + prods[3 + v, t]) + (prods[u + 1, t] + prods[u + v, t])
                    store(top * HALF + low * SUB + t, value)

    def past_products(first, last):
        products(gated_s, tap, first, last, lambda a, m: SUB - 1 + a - m, lambda t: t, False)

    def ahead_products(first, last):
        products(sg_s, tap, first, last, lambda a, m: a + m, lambda t: t, True)

    def lag_products():
        products(gated_s, sg_w, 0, PARTS, lambda a, j: TB - 1 + j - a, lambda t: TB - t, False)

    def store_long(t, value):
        long_n[pl.ds(t, SEGS, stride=PITCH), :] = value

    def store_mixed(t, value):
        mixed_n[pl.ds(t, SEGS, stride=PITCH), :] = value

    def store_fsum(m, value):
        fsum[pl.ds(pl.multiple_of(m * SEGS, SEGS), SEGS), :] = value

    def end_state(source, offset, backward):
        rates = [decay[n] for n in range(MODES)]

        def step(j, state):
            x = source[offset + (SPAN - 1 - j if backward else j)]
            return tuple(rates[n] * state[n] + x for n in range(MODES))

        zero = jnp.zeros((SEGS, LANES), jnp.float32)
        return lax.fori_loop(0, SPAN, step, (zero,) * MODES, unroll=4)

    def segments(backward):
        return range(SEGS - 1, -1, -1) if backward else range(SEGS)

    def share_states(state, ends, states, stage, backward):
        for n in range(MODES):
            ends[n * SEGS : (n + 1) * SEGS, :] = state[n]
        carried = jnp.zeros((MODES, LANES), jnp.float32)
        for s in segments(backward):
            carried = span_decay * carried + ends[pl.ds(s, MODES, stride=SEGS), :]
        states[z] = carried

        @pl.loop(1, planes)
        def _(d):
            push(stage, states.at[z], states.at[z], z_peer(d)[1])

    def entering(ends, states, stage, backward):
        await_bytes(recv.at[stage], states.at[pl.ds(0, planes - 1)])
        carried = jnp.zeros((MODES, LANES), jnp.float32)
        for other in range(planes - 1, -1, -1) if backward else range(planes):
            counts = (other > z) if backward else (other < z)
            carried = jnp.where(counts, plane_decay * carried + states[other], carried)
        for s in segments(backward):
            starts[pl.ds(s, MODES, stride=SEGS), :] = carried
            carried = span_decay * carried + ends[pl.ds(s, MODES, stride=SEGS), :]
        return tuple(starts[n * SEGS : (n + 1) * SEGS, :] for n in range(MODES))

    def run(source, offset, state, backward, emit):
        rates = [decay[n] for n in range(MODES)]

        def step(k, state):
            j = SPAN - 1 - k if backward else k
            x = source[offset + j]
            state = tuple(rates[n] * state[n] + x for n in range(MODES))
            terms = [gain[n] * state[n] for n in range(MODES)]
            while len(terms) > 1:
                terms = [a + b for a, b in zip(terms[::2], terms[1::2])]
            emit(j, terms[0])
            return state

        lax.fori_loop(0, SPAN, step, state, unroll=2)

    def emit_sg(j, y):
        sg[j] = y
        first_sg[pl.ds(j, 1), :] = y[0:1, :]

    def emit_u(j, y):
        u[SPAN + j] = y
        last_u[pl.ds(j, 1), :] = y[SEGS - 1 : SEGS, :]

    def output(stage, scaled_by, values, staged, out, first, count):
        @pl.loop(0, SEGS)
        def _(s):
            start = pl.multiple_of(s * PITCH + first, 8)
            value = values[pl.ds(start, count), :] * scaled_by[s, pl.ds(first, count)].astype(jnp.float32)
            staged[s, pl.ds(first, count)] = value.astype(jnp.bfloat16)

        place = out.at[pl.ds(first, count), mine]

        @pl.loop(1, SEGS)
        def _(d):
            other, device = row_peer(d)
            push(stage, staged.at[other, pl.ds(first, count)], place, device)

        keep(stage, staged.at[i, pl.ds(first, count)], place)

    await_bytes(recv.at[QU], in_qu)
    product(in_qu, grad_n)
    by_segment(grad_n, grad, 0)
    share_states(end_state(grad, 0, True), ends_b, states_b, ST_B, True)

    def move_sublanes(ref, src, dst, by):
        @pl.loop(0, SPAN, unroll=4)
        def _(j):
            ref[dst + j] = pltpu.roll(ref[src + j], by, 0)

    def merge(ref, first, halo, sublane, nothing):
        @pl.loop(0, SPAN, unroll=4)
        def _(j):
            row = jnp.where(nothing, 0.0, halo[pl.ds(j, 1), :])
            row = jnp.broadcast_to(row, (SEGS, LANES))
            ref[first + j] = jnp.where(segment == sublane, row, ref[first + j])

    await_bytes(recv.at[KV], in_kv)
    product(in_kv, gated_n)
    last_gated = gated_n.at[pl.ds((SEGS - 1) * PITCH, SPAN)]
    push(HALO_F, last_gated, past, z_peer(1)[1])
    by_segment(gated_n, gated, SPAN)
    share_states(end_state(gated, SPAN, False), ends_f, states_f, ST_F, False)

    run(grad, 0, entering(ends_b, states_b, ST_B, True), True, emit_sg)
    push(HALO_B, first_sg, future, z_peer(planes - 1)[1])

    @pl.loop(0, SUB)
    def _(j):
        quarters = [sg[j + SUB * s] for s in range(4)]
        for g, value in enumerate(combine_halves(quarters, False)):
            sg_w[g, j] = value

    move_sublanes(gated, SPAN, 0, 1)
    move_sublanes(sg, 0, SPAN, SEGS - 1)
    await_bytes(recv.at[HALO_F], past)
    merge(gated, 0, past, 0, z == 0)
    differences(gated, 1, gated_s)

    lag_products()
    recombine(store_fsum, (0, 1), True)

    @pl.loop(0, TAPS // SEGS)
    def _(b):
        start = b * SEGS * SEGS
        value = fsum[pl.ds(start, SEGS, stride=SEGS), :]
        for s in range(1, SEGS):
            value = value + fsum[pl.ds(start + s, SEGS, stride=SEGS), :]
        taps_t[pl.ds(pl.multiple_of(b * SEGS, SEGS), SEGS), :] = value

    fpart[...] = jnp.transpose(taps_t[...]).reshape(planes, piece, TAPS)
    frecv[z] = fpart[z]

    @pl.loop(1, planes)
    def _(d):
        other, device = z_peer(d)
        push(RS, fpart.at[other], frecv.at[z], device)

    run(gated, SPAN, entering(ends_f, states_f, ST_F, False), False, emit_u)
    push(HALO_U, last_u, past_u, z_peer(1)[1])
    move_sublanes(u, SPAN, 0, 1)

    over_z, over_plane = pl.ds(0, half_piece), pl.ds(half_piece, half_piece)

    def sum_planes():
        await_bytes(recv.at[RS], frecv.at[pl.ds(0, planes - 1)])
        value = frecv[0]
        for other in range(1, planes):
            value = value + frecv[other]
        fmine[...] = value
        z_place, plane_place = fg_out.at[i, z, over_z], fg_out.at[i, z, over_plane]

        @pl.loop(1, planes)
        def _(d):
            push(Z1, fmine.at[over_z], z_place, z_peer(d)[1])

        @pl.loop(1, SEGS)
        def _(d):
            push(P1, fmine.at[over_plane], plane_place, row_peer(d)[1])

        keep(Z1, fmine.at[over_z], z_place)
        keep(P1, fmine.at[over_plane], plane_place)

    def spread():
        await_bytes(recv.at[P1], fg_out.at[:, 0, over_plane])

        @pl.loop(1, planes)
        def _(d):
            place = fg_out.at[:, z, over_plane]
            push(P2, place, place, z_peer(d)[1])

        await_bytes(recv.at[Z1], fg_out.at[0, :, over_z])

        @pl.loop(1, SEGS)
        def _(d):
            place = fg_out.at[i, :, over_z]
            push(Z2, place, place, row_peer(d)[1])

    await_bytes(recv.at[HALO_B], future)
    merge(sg, SPAN, future, SEGS - 1, z == planes - 1)
    differences(sg, 0, sg_s)
    ahead_products(0, 6)
    sum_planes()
    recombine(store_mixed, (0,), False)
    output(OUT_K0, in_kv.at[1], mixed_n, out_k, kg_out, 0, HALF)
    output(OUT_V0, in_kv.at[0], mixed_n, out_v, vg_out, 0, HALF)
    ahead_products(6, PARTS)
    recombine(store_mixed, (1,), False)
    output(OUT_K1, in_kv.at[1], mixed_n, out_k, kg_out, HALF, HALF)
    output(OUT_V1, in_kv.at[0], mixed_n, out_v, vg_out, HALF, HALF)

    await_bytes(recv.at[HALO_U], past_u)
    merge(u, 0, past_u, 0, z == 0)
    differences(u, 1, gated_s)
    past_products(0, 6)
    spread()
    recombine(store_long, (0,), False)
    output(OUT_Q0, in_qu.at[1], long_n, out_q, qg_out, 0, HALF)
    past_products(6, PARTS)
    recombine(store_long, (1,), False)
    output(OUT_Q1, in_qu.at[1], long_n, out_q, qg_out, HALF, HALF)

    low, high = pl.ds(0, HALF), pl.ds(HALF, HALF)
    others = pl.ds(0, SEGS - 1)
    other_planes = pl.ds(0, planes - 1)
    for stage, like in (
        (OUT_Q0, qg_out.at[low]),
        (OUT_Q1, qg_out.at[high]),
        (OUT_K0, kg_out.at[low]),
        (OUT_V0, vg_out.at[low]),
        (Z2, fg_out.at[others, :, over_z]),
        (P2, fg_out.at[:, other_planes, over_plane]),
        (OUT_K1, kg_out.at[high]),
        (OUT_V1, vg_out.at[high]),
    ):
        await_bytes(recv.at[stage], like)
    most = pl.ds(0, SEGS - 1)
    for stage, like in (
        (HALO_F, past),
        (HALO_B, future),
        (HALO_U, past_u),
        (ST_F, states_f.at[other_planes]),
        (ST_B, states_b.at[other_planes]),
        (OUT_Q0, out_q.at[most, low]),
        (OUT_Q1, out_q.at[most, high]),
        (OUT_K0, out_k.at[most, low]),
        (OUT_V0, out_v.at[most, low]),
        (OUT_K1, out_k.at[most, high]),
        (OUT_V1, out_v.at[most, high]),
        (RS, frecv.at[other_planes]),
        (Z1, fg_out.at[0, other_planes, over_z]),
        (P1, fg_out.at[others, 0, over_plane]),
        (Z2, fg_out.at[others, :, over_z]),
        (P2, fg_out.at[:, other_planes, over_plane]),
    ):
        await_bytes(send.at[stage], like)
    for stage, like in ((KV, in_kv), (QU, in_qu)):
        await_bytes(send.at[stage], like.at[:, pl.ds(0, SEGS - 1)])
        if parts > 1:
            await_bytes(send.at[stage], like.at[:, 0, pl.ds(0, SPAN - rows)])


def finish(*refs):
    sources, results, done = refs[:4], refs[4:8], refs[8]
    copies = [
        pltpu.make_async_copy(src, dst, done.at[n])
        for n, (src, dst) in enumerate(zip(sources, results))
    ]
    for copy in copies:
        copy.start()
    for copy in copies:
        copy.wait()


def body(planes, parts, q_gate, key_in, value_in, out_grad, mr_filter, residues, decay_rates):
    piece = TAPS // planes
    f32, bf16 = jnp.float32, jnp.bfloat16

    def vmem(*shape, kind=f32):
        return pltpu.VMEM(shape, kind)

    scratch = [
        vmem(4, *q_gate.shape, kind=bf16),
        vmem(2, SEGS, SPAN, LANES, kind=bf16),
        vmem(2, SEGS, SPAN, LANES, kind=bf16),
        vmem(LANES, TAPS),
        vmem(MODES, LANES),
        vmem(MODES, LANES),
        vmem(TAPS, LANES),
        vmem(PARTS, SUB, SEGS, LANES),
        vmem(MODES, SEGS, LANES),
        vmem(MODES, SEGS, LANES),
        vmem(SEGS * PITCH, LANES),
        vmem(2 * SPAN, SEGS, LANES),
        vmem(PARTS, 2 * SUB, SEGS, LANES),
        vmem(2 * SPAN, SEGS, LANES),
        vmem(SEGS * PITCH, LANES),
        vmem(SPAN, SEGS, LANES),
        vmem(MODES * SEGS, LANES),
        vmem(MODES * SEGS, LANES),
        vmem(MODES * SEGS, LANES),
        vmem(planes, MODES, LANES),
        vmem(planes, MODES, LANES),
        vmem(SEGS * PITCH, LANES),
        vmem(2 * SPAN, SEGS, LANES),
        vmem(PARTS, 2 * SUB, SEGS, LANES),
        vmem(PARTS, SUB, SEGS, LANES),
        vmem(SPAN, LANES),
        vmem(SPAN, LANES),
        vmem(SPAN, LANES),
        vmem(SPAN, LANES),
        vmem(SPAN, LANES),
        vmem(PARTS, SUB, SEGS, LANES),
        vmem(SEGS * PITCH, LANES),
        vmem(SEGS, SPAN, LANES, kind=bf16),
        vmem(SEGS, SPAN, LANES, kind=bf16),
        vmem(SEGS, SPAN, LANES, kind=bf16),
        vmem(TAPS * SEGS, LANES),
        vmem(planes, piece, TAPS),
        vmem(planes, piece, TAPS),
        vmem(piece, TAPS),
        pltpu.SemaphoreType.DMA((STAGES,)),
        pltpu.SemaphoreType.DMA((STAGES,)),
        pltpu.SemaphoreType.DMA((7,)),
    ]
    anywhere = pl.BlockSpec(memory_space=pl.ANY)
    hbm = pl.BlockSpec(memory_space=pltpu.HBM)
    out = jax.ShapeDtypeStruct((SPAN, SEGS * LANES), bf16)
    shapes = (out, out, out, jax.ShapeDtypeStruct((SEGS, planes, piece, TAPS), f32))
    operands = (q_gate, key_in, value_in, out_grad, mr_filter, residues.T, decay_rates.T)
    operands = [pltpu.with_memory_space_constraint(x, pltpu.HBM) for x in operands]
    results = pl.pallas_call(
        functools.partial(kernel, planes, parts),
        out_shape=tuple(pltpu.VMEM(x.shape, x.dtype) for x in shapes),
        in_specs=[hbm] * 7,
        out_specs=(anywhere,) * 4,
        scratch_shapes=scratch,
        compiler_params=pltpu.CompilerParams(
            collective_id=0, has_side_effects=True, vmem_limit_bytes=VMEM
        ),
    )(*operands)
    *grads, filter_grad = pl.pallas_call(
        finish,
        out_shape=tuple(pltpu.HBM(x.shape, x.dtype) for x in shapes),
        in_specs=[anywhere] * 4,
        out_specs=(hbm,) * 4,
        scratch_shapes=[pltpu.SemaphoreType.DMA((4,))],
        compiler_params=pltpu.CompilerParams(vmem_limit_bytes=VMEM),
    )(*results)
    return (*grads, filter_grad.reshape(SEGS * LANES, TAPS))


def solution(mesh):
    rows = P(("seq", "tp"), None)
    return jax.shard_map(
        functools.partial(body, mesh.shape["seq"] // SEGS, mesh.shape["tp"]),
        mesh=mesh,
        in_specs=(rows, rows, rows, rows, P("tp", None), P("tp", None), P("tp", None)),
        out_specs=(P("seq", "tp"), P("seq", "tp"), P("seq", "tp"), P("tp", None)),
        check_vma=False,
    )
```

```python
import functools

import jax
import jax.numpy as jnp
from jax import lax
from jax.experimental import pallas as pl
from jax.experimental.pallas import tpu as pltpu
from jax.sharding import PartitionSpec as P

MESH = pl.DeviceIdType.MESH
SEGS = 8
SPAN = 128
LANES = 128
TAPS = 128
MODES = 16
PLANE = SEGS * SPAN
HALF = SPAN // 2
LEVELS = 3
SUB = TAPS >> LEVELS
PARTS = 3**LEVELS
TOP = PARTS // 3
UNROLL = 3
VMEM = 40 * 1024 * 1024
(KV, QU, HALO_F, HALO_B, HALO_U, ST_F, ST_B, OUT_Q0, OUT_Q1, OUT_K0, OUT_V0, OUT_K1, OUT_V1, RS, Z1, P1, Z2, P2) = range(18)
STAGES = 18
PITCH = SPAN + 8


def hops(step, size):
    return min(step, size - step)


def farthest_first(peers):
    return [step for _, step in sorted((-distance, step) for distance, step in peers)]


def row_steps():
    steps = [(x, y) for x in range(SEGS // 2) for y in range(2) if (x, y) != (0, 0)]
    return farthest_first((hops(x, SEGS // 2) + 2 * y, (x, y)) for x, y in steps)


def plane_steps(parts):
    lows, cores = (2, 2) if parts == 4 else (1, parts)
    steps = [
        (x, y, low, core)
        for core in range(cores)
        for x in range(SEGS // 2)
        for y in range(2)
        for low in range(lows)
    ]
    distance = {(0, 0): 0, (1, 0): 2, (0, 1): 1, (1, 1): 1}
    return farthest_first(
        (hops(step[0], SEGS // 2) + distance[step[1:3]], step) for step in steps if any(step)
    )


def kernel(
    planes,
    parts,
    q_hbm,
    k_hbm,
    v_hbm,
    u_hbm,
    filt_hbm,
    res_hbm,
    dec_hbm,
    qg_out,
    kg_out,
    vg_out,
    fg_out,
    stack,
    in_kv,
    in_qu,
    filt,
    res,
    dec,
    taps_t,
    tap,
    decay,
    gain,
    gated_n,
    gated,
    gated_s,
    u,
    grad_n,
    grad,
    ends_f,
    ends_b,
    starts,
    states_f,
    states_b,
    long_n,
    sg,
    sg_s,
    sg_w,
    past,
    first_sg,
    future,
    last_u,
    past_u,
    prods,
    mixed_n,
    out_q,
    out_k,
    out_v,
    fsum,
    fpart,
    frecv,
    fmine,
    send,
    recv,
    local,
):
    rows = SPAN // parts
    chunks = SEGS * parts
    piece = TAPS // planes
    half_piece = piece // 2
    seq, p = lax.axis_index("seq"), lax.axis_index("tp")
    z, i = seq // SEGS, seq % SEGS

    x, y = lax.div(i, 2), lax.rem(i, 2)
    cores = 2 if parts == 4 else parts
    y_low, core = lax.div(p, cores), lax.rem(p, cores)

    def segment_at(step):
        return lax.rem(x + step[0], SEGS // 2) * 2 + lax.rem(y + step[1], 2)

    def plane_peer(step):
        other = segment_at(step)
        part = lax.rem(y_low + step[2], 2) * cores + lax.rem(core + step[3], cores)
        return other, part, (z * SEGS + other, part)

    def row_peer(step):
        other = segment_at(step)
        return other, (z * SEGS + other, p)

    def z_peer(d):
        other = lax.rem(z + d, planes)
        return other, (other * SEGS + i, p)

    in_plane, in_row = plane_steps(parts), row_steps()
    along_z = sorted(range(1, planes), key=lambda d: -hops(d, planes))

    def push(stage, src, dst, device):
        pltpu.make_async_remote_copy(
            src_ref=src,
            dst_ref=dst,
            send_sem=send.at[stage],
            recv_sem=recv.at[stage],
            device_id=device,
            device_id_type=MESH,
        ).start()

    def keep(stage, src, dst):
        pltpu.make_async_copy(src, dst, recv.at[stage]).start()

    def await_bytes(sem, like):
        pltpu.make_async_copy(like, like, sem).wait()

    barrier = pltpu.get_barrier_semaphore()

    for step in in_plane:
        pl.semaphore_signal(barrier, inc=1, device_id=plane_peer(step)[2], device_id_type=MESH)
    for d in along_z:
        pl.semaphore_signal(barrier, inc=1, device_id=z_peer(d)[1], device_id_type=MESH)

    mine = pl.ds(pl.multiple_of(i * LANES, LANES), LANES)
    loads = [
        pltpu.make_async_copy(src, stack.at[n], local.at[n])
        for n, src in enumerate((k_hbm, v_hbm, q_hbm, u_hbm))
    ]
    params = [
        pltpu.make_async_copy(filt_hbm.at[mine], filt, local.at[4]),
        pltpu.make_async_copy(res_hbm.at[:, mine], res, local.at[5]),
        pltpu.make_async_copy(dec_hbm.at[:, mine], dec, local.at[6]),
    ]
    for copy in loads + params:
        copy.start()
    for copy in loads:
        copy.wait()
    pl.semaphore_wait(barrier, chunks - 1 + planes - 1)

    def columns(segment, part):
        return pl.ds(pl.multiple_of(part * PLANE + segment * LANES, LANES), LANES)

    own_rows = pl.ds(pl.multiple_of(p * rows, rows), rows)

    def scatter(stage, first, dst):
        for step in in_plane:
            segment, part, device = plane_peer(step)
            src = stack.at[pl.ds(first, 2), :, columns(segment, part)]
            push(stage, src, dst.at[:, i, own_rows], device)

        keep(stage, stack.at[pl.ds(first, 2), :, columns(i, p)], dst.at[:, i, own_rows])

    scatter(QU, 2, in_qu)
    scatter(KV, 0, in_kv)

    for copy in params:
        copy.wait()
    taps_t[...] = jnp.transpose(filt[...])

    def combine_halves(pieces, swapped):
        if len(pieces) == 1:
            return pieces
        half = len(pieces) // 2
        low, high = pieces[:half], pieces[half:]
        both = [x + y for x, y in zip(low, high)]
        order = (high, both, low) if swapped else (low, both, high)
        return sum((combine_halves(part, swapped) for part in order), [])

    @pl.loop(0, SUB)
    def _(m):
        pieces = [
            jnp.broadcast_to(taps_t[pl.ds(m + s, 1), :], (SEGS, LANES)) for s in range(0, TAPS, SUB)
        ]
        for g, value in enumerate(combine_halves(pieces, True)):
            tap[g, m] = value

    @pl.loop(0, MODES)
    def _(n):
        rate = jnp.broadcast_to(dec[pl.ds(n, 1), :], (SEGS, LANES))
        weight = jnp.broadcast_to(res[pl.ds(n, 1), :], (SEGS, LANES))
        u = 2.0 * rate
        series = jnp.ones_like(u)
        for order in range(8, 1, -1):
            series = 1.0 - (u * (1.0 / order)) * series
        decay[n] = jnp.exp(-rate)
        gain[n] = weight * jnp.sqrt(u * series)

    span_decay = jnp.exp(-float(SPAN) * dec[...])
    plane_decay = jnp.exp(-float(PLANE) * dec[...])

    segment = lax.broadcasted_iota(jnp.int32, (SEGS, LANES), 0)

    def product(pair, dst, first, last):
        @pl.loop(first, last)
        def _(s):
            value = pair[0, s].astype(jnp.float32) * pair[1, s].astype(jnp.float32)
            dst[pl.ds(pl.multiple_of(s * PITCH, 8), SPAN), :] = value

    def by_segment(source, dst, first):
        @pl.loop(0, SPAN, unroll=4)
        def _(j):
            dst[first + j] = source[pl.ds(j, SEGS, stride=PITCH), :]

    def split(pieces):
        if len(pieces) == 1:
            return pieces
        step = (len(pieces) + 1) // 4
        before, middle, after = (pieces[s : s + 2 * step - 1] for s in (0, step, 2 * step))
        before = [x - y for x, y in zip(before, middle)]
        after = [x - y for x, y in zip(after, middle)]
        return split(before) + split(middle) + split(after)

    def differences(source, first, dst):
        @pl.loop(0, 2 * SUB - 1)
        def _(k):
            pieces = [source[first + k + s] for s in range(0, 2 * TAPS - SUB, SUB)]
            for g, value in enumerate(split(pieces)):
                dst[g, k] = value

    def products(gen, vec, first, last, place, swapped):
        @pl.loop(first, last, unroll=UNROLL)
        def _(g):
            window = gen[g]
            weights = vec[PARTS - 1 - g if swapped else g]
            acc = [jnp.zeros((SEGS, LANES), jnp.float32) for _ in range(SUB)]
            for m in range(SUB):
                for t in range(SUB):
                    acc[t] = acc[t] + weights[m] * window[place(t, m)]
            for t in range(SUB):
                prods[g, t] = acc[t]

    def recombine(store, halves, swapped):
        @pl.loop(0, SUB)
        def _(t):
            def outputs_of(first, size, wanted):
                if size == 1:
                    return [prods[first, t]]
                third = size // 3
                middle = outputs_of(first + third, third, (0, 1))
                result = []
                for half in wanted:
                    side = 1 - half if swapped else half
                    outer = outputs_of(first + 2 * third * side, third, (0, 1))
                    result += [x + y for x, y in zip(middle, outer)]
                return result

            for half in halves:
                for n, value in enumerate(outputs_of(0, PARTS, (half,))):
                    store(half * HALF + n * SUB + t, value)

    def past_products(first, last):
        products(gated_s, tap, first, last, lambda t, m: SUB - 1 + t - m, False)

    def ahead_products(first, last):
        products(sg_s, tap, first, last, lambda t, m: t + m, True)

    def lag_products():
        products(gated_s, sg_w, 0, PARTS, lambda m, t: SUB - 1 + t - m, False)

    def store_long(t, value):
        long_n[pl.ds(t, SEGS, stride=PITCH), :] = value

    def store_mixed(t, value):
        mixed_n[pl.ds(t, SEGS, stride=PITCH), :] = value

    def store_fsum(m, value):
        fsum[pl.ds(pl.multiple_of(m * SEGS, SEGS), SEGS), :] = value

    def end_state(source, offset, backward):
        rates = [decay[n] for n in range(MODES)]

        def step(j, state):
            x = source[offset + (SPAN - 1 - j if backward else j)]
            return tuple(rates[n] * state[n] + x for n in range(MODES))

        zero = jnp.zeros((SEGS, LANES), jnp.float32)
        return lax.fori_loop(0, SPAN, step, (zero,) * MODES, unroll=4)

    def segments(backward):
        return range(SEGS - 1, -1, -1) if backward else range(SEGS)

    def share_states(state, ends, states, stage, backward):
        for n in range(MODES):
            ends[n * SEGS : (n + 1) * SEGS, :] = state[n]
        carried = jnp.zeros((MODES, LANES), jnp.float32)
        for s in segments(backward):
            carried = span_decay * carried + ends[pl.ds(s, MODES, stride=SEGS), :]
        states[z] = carried

        for d in along_z:
            push(stage, states.at[z], states.at[z], z_peer(d)[1])

    def entering(ends, states, stage, backward):
        await_bytes(recv.at[stage], states.at[pl.ds(0, planes - 1)])
        carried = jnp.zeros((MODES, LANES), jnp.float32)
        for other in range(planes - 1, -1, -1) if backward else range(planes):
            counts = (other > z) if backward else (other < z)
            carried = jnp.where(counts, plane_decay * carried + states[other], carried)
        for s in segments(backward):
            starts[pl.ds(s, MODES, stride=SEGS), :] = carried
            carried = span_decay * carried + ends[pl.ds(s, MODES, stride=SEGS), :]
        return tuple(starts[n * SEGS : (n + 1) * SEGS, :] for n in range(MODES))

    def run(source, offset, state, backward, emit):
        rates = [decay[n] for n in range(MODES)]

        def step(k, state):
            j = SPAN - 1 - k if backward else k
            x = source[offset + j]
            state = tuple(rates[n] * state[n] + x for n in range(MODES))
            terms = [gain[n] * state[n] for n in range(MODES)]
            while len(terms) > 1:
                terms = [a + b for a, b in zip(terms[::2], terms[1::2])]
            emit(j, terms[0])
            return state

        lax.fori_loop(0, SPAN, step, state, unroll=2)

    def emit_sg(j, y):
        sg[j] = y
        first_sg[pl.ds(j, 1), :] = y[0:1, :]

    def emit_u(j, y):
        u[SPAN + j] = y
        last_u[pl.ds(j, 1), :] = y[SEGS - 1 : SEGS, :]

    def output(stage, scaled_by, values, staged, out, first, count):
        @pl.loop(0, SEGS)
        def _(s):
            start = pl.multiple_of(s * PITCH + first, 8)
            value = values[pl.ds(start, count), :] * scaled_by[s, pl.ds(first, count)].astype(jnp.float32)
            staged[s, pl.ds(first, count)] = value.astype(jnp.bfloat16)

        place = out.at[pl.ds(first, count), mine]

        for step in in_row:
            other, device = row_peer(step)
            push(stage, staged.at[other, pl.ds(first, count)], place, device)

        keep(stage, staged.at[i, pl.ds(first, count)], place)

    await_bytes(recv.at[QU], in_qu)
    product(in_qu, grad_n, 0, SEGS)
    by_segment(grad_n, grad, 0)
    share_states(end_state(grad, 0, True), ends_b, states_b, ST_B, True)

    def move_sublanes(ref, src, dst, by):
        @pl.loop(0, SPAN, unroll=4)
        def _(j):
            ref[dst + j] = pltpu.roll(ref[src + j], by, 0)

    def merge(ref, first, halo, sublane, nothing):
        @pl.loop(0, SPAN, unroll=4)
        def _(j):
            row = jnp.where(nothing, 0.0, halo[pl.ds(j, 1), :])
            row = jnp.broadcast_to(row, (SEGS, LANES))
            ref[first + j] = jnp.where(segment == sublane, row, ref[first + j])

    await_bytes(recv.at[KV], in_kv)
    product(in_kv, gated_n, SEGS - 1, SEGS)
    last_gated = gated_n.at[pl.ds((SEGS - 1) * PITCH, SPAN)]
    push(HALO_F, last_gated, past, z_peer(1)[1])
    product(in_kv, gated_n, 0, SEGS - 1)
    by_segment(gated_n, gated, SPAN)
    share_states(end_state(gated, SPAN, False), ends_f, states_f, ST_F, False)

    run(grad, 0, entering(ends_b, states_b, ST_B, True), True, emit_sg)
    push(HALO_B, first_sg, future, z_peer(planes - 1)[1])

    @pl.loop(0, SUB)
    def _(j):
        pieces = [sg[j + s] for s in range(0, SPAN, SUB)]
        for g, value in enumerate(combine_halves(pieces, False)):
            sg_w[g, j] = value

    move_sublanes(gated, SPAN, 0, 1)
    move_sublanes(sg, 0, SPAN, SEGS - 1)
    await_bytes(recv.at[HALO_F], past)
    merge(gated, 0, past, 0, z == 0)
    differences(gated, 1, gated_s)

    lag_products()
    recombine(store_fsum, (0, 1), True)

    @pl.loop(0, TAPS // SEGS)
    def _(b):
        start = b * SEGS * SEGS
        value = fsum[pl.ds(start, SEGS, stride=SEGS), :]
        for s in range(1, SEGS):
            value = value + fsum[pl.ds(start + s, SEGS, stride=SEGS), :]
        taps_t[pl.ds(pl.multiple_of(b * SEGS, SEGS), SEGS), :] = value

    fpart[...] = jnp.transpose(taps_t[...]).reshape(planes, piece, TAPS)
    frecv[z] = fpart[z]

    for d in along_z:
        other, device = z_peer(d)
        push(RS, fpart.at[other], frecv.at[z], device)

    run(gated, SPAN, entering(ends_f, states_f, ST_F, False), False, emit_u)
    push(HALO_U, last_u, past_u, z_peer(1)[1])
    move_sublanes(u, SPAN, 0, 1)

    over_z, over_plane = pl.ds(0, half_piece), pl.ds(half_piece, half_piece)

    def sum_planes():
        await_bytes(recv.at[RS], frecv.at[pl.ds(0, planes - 1)])
        value = frecv[0]
        for other in range(1, planes):
            value = value + frecv[other]
        fmine[...] = value
        z_place, plane_place = fg_out.at[i, z, over_z], fg_out.at[i, z, over_plane]

        for d in along_z:
            push(Z1, fmine.at[over_z], z_place, z_peer(d)[1])

        for step in in_row:
            push(P1, fmine.at[over_plane], plane_place, row_peer(step)[1])

        keep(Z1, fmine.at[over_z], z_place)
        keep(P1, fmine.at[over_plane], plane_place)

    def spread():
        await_bytes(recv.at[P1], fg_out.at[:, 0, over_plane])

        for d in along_z:
            place = fg_out.at[:, z, over_plane]
            push(P2, place, place, z_peer(d)[1])

        await_bytes(recv.at[Z1], fg_out.at[0, :, over_z])

        for step in in_row:
            place = fg_out.at[i, :, over_z]
            push(Z2, place, place, row_peer(step)[1])

    await_bytes(recv.at[HALO_B], future)
    merge(sg, SPAN, future, SEGS - 1, z == planes - 1)
    differences(sg, 0, sg_s)
    ahead_products(0, 2 * TOP)
    sum_planes()
    recombine(store_mixed, (0,), False)
    output(OUT_K0, in_kv.at[1], mixed_n, out_k, kg_out, 0, HALF)
    output(OUT_V0, in_kv.at[0], mixed_n, out_v, vg_out, 0, HALF)
    ahead_products(2 * TOP, PARTS)
    recombine(store_mixed, (1,), False)
    output(OUT_K1, in_kv.at[1], mixed_n, out_k, kg_out, HALF, HALF)
    output(OUT_V1, in_kv.at[0], mixed_n, out_v, vg_out, HALF, HALF)

    await_bytes(recv.at[HALO_U], past_u)
    merge(u, 0, past_u, 0, z == 0)
    differences(u, 1, gated_s)
    past_products(0, 2 * TOP)
    recombine(store_long, (0,), False)
    output(OUT_Q0, in_qu.at[1], long_n, out_q, qg_out, 0, HALF)
    past_products(2 * TOP, PARTS)
    recombine(store_long, (1,), False)
    output(OUT_Q1, in_qu.at[1], long_n, out_q, qg_out, HALF, HALF)
    spread()

    low, high = pl.ds(0, HALF), pl.ds(HALF, HALF)
    others = pl.ds(0, SEGS - 1)
    other_planes = pl.ds(0, planes - 1)
    for stage, like in (
        (OUT_Q0, qg_out.at[low]),
        (OUT_Q1, qg_out.at[high]),
        (OUT_K0, kg_out.at[low]),
        (OUT_V0, vg_out.at[low]),
        (Z2, fg_out.at[others, :, over_z]),
        (P2, fg_out.at[:, other_planes, over_plane]),
        (OUT_K1, kg_out.at[high]),
        (OUT_V1, vg_out.at[high]),
    ):
        await_bytes(recv.at[stage], like)
    most = pl.ds(0, SEGS - 1)
    for stage, like in (
        (HALO_F, past),
        (HALO_B, future),
        (HALO_U, past_u),
        (ST_F, states_f.at[other_planes]),
        (ST_B, states_b.at[other_planes]),
        (OUT_Q0, out_q.at[most, low]),
        (OUT_Q1, out_q.at[most, high]),
        (OUT_K0, out_k.at[most, low]),
        (OUT_V0, out_v.at[most, low]),
        (OUT_K1, out_k.at[most, high]),
        (OUT_V1, out_v.at[most, high]),
        (RS, frecv.at[other_planes]),
        (Z1, fg_out.at[0, other_planes, over_z]),
        (P1, fg_out.at[others, 0, over_plane]),
        (Z2, fg_out.at[others, :, over_z]),
        (P2, fg_out.at[:, other_planes, over_plane]),
    ):
        await_bytes(send.at[stage], like)
    for stage, like in ((KV, in_kv), (QU, in_qu)):
        await_bytes(send.at[stage], like.at[:, pl.ds(0, SEGS - 1)])
        if parts > 1:
            await_bytes(send.at[stage], like.at[:, 0, pl.ds(0, SPAN - rows)])


def finish(*refs):
    sources, results, done = refs[:4], refs[4:8], refs[8]
    copies = [
        pltpu.make_async_copy(src.at[rows], dst.at[rows], done.at[n, c])
        for n, (src, dst) in enumerate(zip(sources, results))
        for c, rows in enumerate(pl.ds(src.shape[0] // 4 * c, src.shape[0] // 4) for c in range(4))
    ]
    for copy in copies:
        copy.start()
    for copy in copies:
        copy.wait()


def body(planes, parts, q_gate, key_in, value_in, out_grad, mr_filter, residues, decay_rates):
    piece = TAPS // planes
    f32, bf16 = jnp.float32, jnp.bfloat16

    def vmem(*shape, kind=f32):
        return pltpu.VMEM(shape, kind)

    scratch = [
        vmem(4, *q_gate.shape, kind=bf16),
        vmem(2, SEGS, SPAN, LANES, kind=bf16),
        vmem(2, SEGS, SPAN, LANES, kind=bf16),
        vmem(LANES, TAPS),
        vmem(MODES, LANES),
        vmem(MODES, LANES),
        vmem(TAPS, LANES),
        vmem(PARTS, SUB, SEGS, LANES),
        vmem(MODES, SEGS, LANES),
        vmem(MODES, SEGS, LANES),
        vmem(SEGS * PITCH, LANES),
        vmem(2 * SPAN, SEGS, LANES),
        vmem(PARTS, 2 * SUB, SEGS, LANES),
        vmem(2 * SPAN, SEGS, LANES),
        vmem(SEGS * PITCH, LANES),
        vmem(SPAN, SEGS, LANES),
        vmem(MODES * SEGS, LANES),
        vmem(MODES * SEGS, LANES),
        vmem(MODES * SEGS, LANES),
        vmem(planes, MODES, LANES),
        vmem(planes, MODES, LANES),
        vmem(SEGS * PITCH, LANES),
        vmem(2 * SPAN, SEGS, LANES),
        vmem(PARTS, 2 * SUB, SEGS, LANES),
        vmem(PARTS, SUB, SEGS, LANES),
        vmem(SPAN, LANES),
        vmem(SPAN, LANES),
        vmem(SPAN, LANES),
        vmem(SPAN, LANES),
        vmem(SPAN, LANES),
        vmem(PARTS, SUB, SEGS, LANES),
        vmem(SEGS * PITCH, LANES),
        vmem(SEGS, SPAN, LANES, kind=bf16),
        vmem(SEGS, SPAN, LANES, kind=bf16),
        vmem(SEGS, SPAN, LANES, kind=bf16),
        vmem(TAPS * SEGS, LANES),
        vmem(planes, piece, TAPS),
        vmem(planes, piece, TAPS),
        vmem(piece, TAPS),
        pltpu.SemaphoreType.DMA((STAGES,)),
        pltpu.SemaphoreType.DMA((STAGES,)),
        pltpu.SemaphoreType.DMA((7,)),
    ]
    anywhere = pl.BlockSpec(memory_space=pl.ANY)
    hbm = pl.BlockSpec(memory_space=pltpu.HBM)
    out = jax.ShapeDtypeStruct((SPAN, SEGS * LANES), bf16)
    shapes = (out, out, out, jax.ShapeDtypeStruct((SEGS, planes, piece, TAPS), f32))
    operands = (q_gate, key_in, value_in, out_grad, mr_filter, residues.T, decay_rates.T)
    operands = [pltpu.with_memory_space_constraint(x, pltpu.HBM) for x in operands]
    results = pl.pallas_call(
        functools.partial(kernel, planes, parts),
        out_shape=tuple(pltpu.VMEM(x.shape, x.dtype) for x in shapes),
        in_specs=[hbm] * 7,
        out_specs=(anywhere,) * 4,
        scratch_shapes=scratch,
        compiler_params=pltpu.CompilerParams(
            collective_id=0, has_side_effects=True, vmem_limit_bytes=VMEM
        ),
    )(*operands)
    *grads, filter_grad = pl.pallas_call(
        finish,
        out_shape=tuple(pltpu.HBM(x.shape, x.dtype) for x in shapes),
        in_specs=[anywhere] * 4,
        out_specs=(hbm,) * 4,
        scratch_shapes=[pltpu.SemaphoreType.DMA((4, 4))],
        compiler_params=pltpu.CompilerParams(vmem_limit_bytes=VMEM),
    )(*results)
    return (*grads, filter_grad.reshape(SEGS * LANES, TAPS))


def solution(mesh):
    rows = P(("seq", "tp"), None)
    return jax.shard_map(
        functools.partial(body, mesh.shape["seq"] // SEGS, mesh.shape["tp"]),
        mesh=mesh,
        in_specs=(rows, rows, rows, rows, P("tp", None), P("tp", None), P("tp", None)),
        out_specs=(P("seq", "tp"), P("seq", "tp"), P("seq", "tp"), P("tp", None)),
        check_vma=False,
    )
```

```python
import functools

import jax
import jax.numpy as jnp
from jax import lax
from jax.experimental import pallas as pl
from jax.experimental.pallas import tpu as pltpu
from jax.sharding import PartitionSpec as P

MESH = pl.DeviceIdType.MESH
SEGS = 8
SPAN = 128
LANES = 128
TAPS = 128
MODES = 16
PLANE = SEGS * SPAN
HALF = SPAN // 2
LEVELS = 3
SUB = TAPS >> LEVELS
PARTS = 3**LEVELS
TOP = PARTS // 3
UNROLL = 9
VMEM = 40 * 1024 * 1024
(KV, QU, HALO_F, HALO_B, HALO_U, ST_F, ST_B, OUT_Q0, OUT_Q1, OUT_KV0, OUT_KV1, RS, Z1, P1, Z2, P2) = range(16)
STAGES = 16
PITCH = SPAN + 8


def hops(step, size):
    return min(step, size - step)


def farthest_first(peers):
    return [step for _, step in sorted((-distance, step) for distance, step in peers)]


def row_steps():
    steps = [(x, y) for x in range(SEGS // 2) for y in range(2) if (x, y) != (0, 0)]
    return farthest_first((hops(x, SEGS // 2) + 2 * y, (x, y)) for x, y in steps)


def plane_steps(parts):
    lows, cores = (2, 2) if parts == 4 else (1, parts)
    steps = [
        (x, y, low, core)
        for core in range(cores)
        for x in range(SEGS // 2)
        for y in range(2)
        for low in range(lows)
    ]
    distance = {(0, 0): 0, (1, 0): 2, (0, 1): 1, (1, 1): 1}
    return farthest_first(
        (hops(step[0], SEGS // 2) + distance[step[1:3]], step) for step in steps if any(step)
    )


def kernel(
    planes,
    parts,
    q_hbm,
    k_hbm,
    v_hbm,
    u_hbm,
    filt_hbm,
    res_hbm,
    dec_hbm,
    qg_out,
    kvg_out,
    fg_out,
    stack,
    in_kv,
    in_qu,
    filt,
    res,
    dec,
    taps_t,
    tap,
    decay,
    gain,
    gated_n,
    gated,
    gated_s,
    u,
    grad_n,
    grad,
    ends_f,
    ends_b,
    starts,
    states_f,
    states_b,
    long_n,
    sg,
    sg_s,
    sg_w,
    past,
    first_sg,
    future,
    last_u,
    past_u,
    prods,
    mixed_n,
    out_q,
    out_kv,
    fsum,
    fpart,
    frecv,
    fmine,
    send,
    recv,
    local,
):
    rows = SPAN // parts
    chunks = SEGS * parts
    piece = TAPS // planes
    half_piece = piece // 2
    seq, p = lax.axis_index("seq"), lax.axis_index("tp")
    z, i = seq // SEGS, seq % SEGS

    x, y = lax.div(i, 2), lax.rem(i, 2)
    cores = 2 if parts == 4 else parts
    y_low, core = lax.div(p, cores), lax.rem(p, cores)

    def segment_at(step):
        return lax.rem(x + step[0], SEGS // 2) * 2 + lax.rem(y + step[1], 2)

    def plane_peer(step):
        other = segment_at(step)
        part = lax.rem(y_low + step[2], 2) * cores + lax.rem(core + step[3], cores)
        return other, part, (z * SEGS + other, part)

    def row_peer(step):
        other = segment_at(step)
        return other, (z * SEGS + other, p)

    def z_peer(d):
        other = lax.rem(z + d, planes)
        return other, (other * SEGS + i, p)

    in_plane, in_row = plane_steps(parts), row_steps()
    along_z = sorted(range(1, planes), key=lambda d: -hops(d, planes))

    def push(stage, src, dst, device):
        pltpu.make_async_remote_copy(
            src_ref=src,
            dst_ref=dst,
            send_sem=send.at[stage],
            recv_sem=recv.at[stage],
            device_id=device,
            device_id_type=MESH,
        ).start()

    def keep(stage, src, dst):
        pltpu.make_async_copy(src, dst, recv.at[stage]).start()

    def await_bytes(sem, like):
        pltpu.make_async_copy(like, like, sem).wait()

    barrier = pltpu.get_barrier_semaphore()

    for step in in_plane:
        pl.semaphore_signal(barrier, inc=1, device_id=plane_peer(step)[2], device_id_type=MESH)
    for d in along_z:
        pl.semaphore_signal(barrier, inc=1, device_id=z_peer(d)[1], device_id_type=MESH)

    mine = pl.ds(pl.multiple_of(i * LANES, LANES), LANES)
    loads = [
        pltpu.make_async_copy(src, stack.at[n], local.at[n])
        for n, src in enumerate((k_hbm, v_hbm, q_hbm, u_hbm))
    ]
    params = [
        pltpu.make_async_copy(filt_hbm.at[mine], filt, local.at[4]),
        pltpu.make_async_copy(res_hbm.at[:, mine], res, local.at[5]),
        pltpu.make_async_copy(dec_hbm.at[:, mine], dec, local.at[6]),
    ]
    for copy in loads + params:
        copy.start()
    for copy in loads:
        copy.wait()
    pl.semaphore_wait(barrier, chunks - 1 + planes - 1)

    def columns(segment, part):
        return pl.ds(pl.multiple_of(part * PLANE + segment * LANES, LANES), LANES)

    own_rows = pl.ds(pl.multiple_of(p * rows, rows), rows)

    def scatter(stage, first, dst):
        for step in in_plane:
            segment, part, device = plane_peer(step)
            src = stack.at[pl.ds(first, 2), :, columns(segment, part)]
            push(stage, src, dst.at[:, i, own_rows], device)

        keep(stage, stack.at[pl.ds(first, 2), :, columns(i, p)], dst.at[:, i, own_rows])

    scatter(QU, 2, in_qu)
    scatter(KV, 0, in_kv)

    for copy in params:
        copy.wait()
    taps_t[...] = jnp.transpose(filt[...])

    def combine_halves(pieces, swapped):
        if len(pieces) == 1:
            return pieces
        half = len(pieces) // 2
        low, high = pieces[:half], pieces[half:]
        both = [x + y for x, y in zip(low, high)]
        order = (high, both, low) if swapped else (low, both, high)
        return sum((combine_halves(part, swapped) for part in order), [])

    @pl.loop(0, SUB)
    def _(m):
        pieces = [
            jnp.broadcast_to(taps_t[pl.ds(m + s, 1), :], (SEGS, LANES)) for s in range(0, TAPS, SUB)
        ]
        for g, value in enumerate(combine_halves(pieces, True)):
            tap[g, m] = value

    @pl.loop(0, MODES)
    def _(n):
        rate = jnp.broadcast_to(dec[pl.ds(n, 1), :], (SEGS, LANES))
        weight = jnp.broadcast_to(res[pl.ds(n, 1), :], (SEGS, LANES))
        u = 2.0 * rate
        series = jnp.ones_like(u)
        for order in range(8, 1, -1):
            series = 1.0 - (u * (1.0 / order)) * series
        decay[n] = jnp.exp(-rate)
        gain[n] = weight * jnp.sqrt(u * series)

    span_decay = jnp.exp(-float(SPAN) * dec[...])
    plane_decay = jnp.exp(-float(PLANE) * dec[...])

    segment = lax.broadcasted_iota(jnp.int32, (SEGS, LANES), 0)

    def product(pair, dst, first, last):
        @pl.loop(first, last)
        def _(s):
            value = pair[0, s].astype(jnp.float32) * pair[1, s].astype(jnp.float32)
            dst[pl.ds(pl.multiple_of(s * PITCH, 8), SPAN), :] = value

    def by_segment(source, dst, first):
        @pl.loop(0, SPAN, unroll=4)
        def _(j):
            dst[first + j] = source[pl.ds(j, SEGS, stride=PITCH), :]

    def split(pieces):
        if len(pieces) == 1:
            return pieces
        step = (len(pieces) + 1) // 4
        before, middle, after = (pieces[s : s + 2 * step - 1] for s in (0, step, 2 * step))
        before = [x - y for x, y in zip(before, middle)]
        after = [x - y for x, y in zip(after, middle)]
        return split(before) + split(middle) + split(after)

    def differences(source, first, dst):
        @pl.loop(0, 2 * SUB - 1)
        def _(k):
            pieces = [source[first + k + s] for s in range(0, 2 * TAPS - SUB, SUB)]
            for g, value in enumerate(split(pieces)):
                dst[g, k] = value

    def products(gen, vec, first, last, place, swapped):
        @pl.loop(first, last, unroll=UNROLL)
        def _(g):
            window = gen[g]
            weights = vec[PARTS - 1 - g if swapped else g]
            acc = [jnp.zeros((SEGS, LANES), jnp.float32) for _ in range(SUB)]
            for m in range(SUB):
                for t in range(SUB):
                    acc[t] = acc[t] + weights[m] * window[place(t, m)]
            for t in range(SUB):
                prods[g, t] = acc[t]

    def recombine(store, halves, swapped):
        @pl.loop(0, SUB, unroll=2)
        def _(t):
            def outputs_of(first, size, wanted):
                if size == 1:
                    return [prods[first, t]]
                third = size // 3
                middle = outputs_of(first + third, third, (0, 1))
                result = []
                for half in wanted:
                    side = 1 - half if swapped else half
                    outer = outputs_of(first + 2 * third * side, third, (0, 1))
                    result += [x + y for x, y in zip(middle, outer)]
                return result

            for half in halves:
                for n, value in enumerate(outputs_of(0, PARTS, (half,))):
                    store(half * HALF + n * SUB + t, value)

    def past_products(first, last):
        products(gated_s, tap, first, last, lambda t, m: SUB - 1 + t - m, False)

    def ahead_products(first, last):
        products(sg_s, tap, first, last, lambda t, m: t + m, True)

    def lag_products():
        products(gated_s, sg_w, 0, PARTS, lambda m, t: SUB - 1 + t - m, False)

    def store_long(t, value):
        long_n[pl.ds(t, SEGS, stride=PITCH), :] = value

    def store_mixed(t, value):
        mixed_n[pl.ds(t, SEGS, stride=PITCH), :] = value

    def store_fsum(m, value):
        fsum[pl.ds(pl.multiple_of(m * SEGS, SEGS), SEGS), :] = value

    def end_state(source, offset, backward):
        rates = [decay[n] for n in range(MODES)]

        def step(j, state):
            x = source[offset + (SPAN - 1 - j if backward else j)]
            return tuple(rates[n] * state[n] + x for n in range(MODES))

        zero = jnp.zeros((SEGS, LANES), jnp.float32)
        return lax.fori_loop(0, SPAN, step, (zero,) * MODES, unroll=8)

    def segments(backward):
        return range(SEGS - 1, -1, -1) if backward else range(SEGS)

    def share_states(state, ends, states, stage, backward):
        for n in range(MODES):
            ends[n * SEGS : (n + 1) * SEGS, :] = state[n]
        carried = jnp.zeros((MODES, LANES), jnp.float32)
        for s in segments(backward):
            carried = span_decay * carried + ends[pl.ds(s, MODES, stride=SEGS), :]
        states[z] = carried

        for d in along_z:
            push(stage, states.at[z], states.at[z], z_peer(d)[1])

    def entering(ends, states, stage, backward):
        await_bytes(recv.at[stage], states.at[pl.ds(0, planes - 1)])
        carried = jnp.zeros((MODES, LANES), jnp.float32)
        for other in range(planes - 1, -1, -1) if backward else range(planes):
            counts = (other > z) if backward else (other < z)
            carried = jnp.where(counts, plane_decay * carried + states[other], carried)
        for s in segments(backward):
            starts[pl.ds(s, MODES, stride=SEGS), :] = carried
            carried = span_decay * carried + ends[pl.ds(s, MODES, stride=SEGS), :]
        return tuple(starts[n * SEGS : (n + 1) * SEGS, :] for n in range(MODES))

    def run(source, offset, state, backward, emit):
        rates = [decay[n] for n in range(MODES)]

        def step(k, state):
            j = SPAN - 1 - k if backward else k
            x = source[offset + j]
            state = tuple(rates[n] * state[n] + x for n in range(MODES))
            terms = [gain[n] * state[n] for n in range(MODES)]
            while len(terms) > 1:
                terms = [a + b for a, b in zip(terms[::2], terms[1::2])]
            emit(j, terms[0])
            return state

        lax.fori_loop(0, SPAN, step, state, unroll=4)

    def emit_sg(j, y):
        sg[j] = y
        first_sg[pl.ds(j, 1), :] = y[0:1, :]

    def emit_u(j, y):
        u[SPAN + j] = y
        last_u[pl.ds(j, 1), :] = y[SEGS - 1 : SEGS, :]

    def output(stage, factors, values, staged, out, first, count):
        @pl.loop(0, SEGS, unroll=2)
        def _(s):
            value = values[pl.ds(pl.multiple_of(s * PITCH + first, 8), count), :]
            for n, factor in enumerate(factors):
                scaled = value * factor[s, pl.ds(first, count)].astype(jnp.float32)
                staged[n, s, pl.ds(first, count)] = scaled.astype(jnp.bfloat16)

        place = out.at[:, pl.ds(first, count), mine]
        for step in in_row:
            other, device = row_peer(step)
            push(stage, staged.at[:, other, pl.ds(first, count)], place, device)

        keep(stage, staged.at[:, i, pl.ds(first, count)], place)

    await_bytes(recv.at[QU], in_qu)
    product(in_qu, grad_n, 0, SEGS)
    by_segment(grad_n, grad, 0)
    share_states(end_state(grad, 0, True), ends_b, states_b, ST_B, True)

    def move_sublanes(ref, src, dst, by):
        @pl.loop(0, SPAN, unroll=4)
        def _(j):
            ref[dst + j] = pltpu.roll(ref[src + j], by, 0)

    def merge(ref, first, halo, sublane, nothing):
        @pl.loop(0, SPAN, unroll=4)
        def _(j):
            row = jnp.where(nothing, 0.0, halo[pl.ds(j, 1), :])
            row = jnp.broadcast_to(row, (SEGS, LANES))
            ref[first + j] = jnp.where(segment == sublane, row, ref[first + j])

    await_bytes(recv.at[KV], in_kv)
    product(in_kv, gated_n, SEGS - 1, SEGS)
    last_gated = gated_n.at[pl.ds((SEGS - 1) * PITCH, SPAN)]
    push(HALO_F, last_gated, past, z_peer(1)[1])
    product(in_kv, gated_n, 0, SEGS - 1)
    by_segment(gated_n, gated, SPAN)
    share_states(end_state(gated, SPAN, False), ends_f, states_f, ST_F, False)

    run(grad, 0, entering(ends_b, states_b, ST_B, True), True, emit_sg)
    push(HALO_B, first_sg, future, z_peer(planes - 1)[1])

    @pl.loop(0, SUB, unroll=2)
    def _(j):
        pieces = [sg[j + s] for s in range(0, SPAN, SUB)]
        for g, value in enumerate(combine_halves(pieces, False)):
            sg_w[g, j] = value

    move_sublanes(gated, SPAN, 0, 1)
    move_sublanes(sg, 0, SPAN, SEGS - 1)
    await_bytes(recv.at[HALO_F], past)
    merge(gated, 0, past, 0, z == 0)
    differences(gated, 1, gated_s)

    lag_products()
    recombine(store_fsum, (0, 1), True)

    @pl.loop(0, TAPS // SEGS, unroll=4)
    def _(b):
        start = b * SEGS * SEGS
        value = fsum[pl.ds(start, SEGS, stride=SEGS), :]
        for s in range(1, SEGS):
            value = value + fsum[pl.ds(start + s, SEGS, stride=SEGS), :]
        taps_t[pl.ds(pl.multiple_of(b * SEGS, SEGS), SEGS), :] = value

    fpart[...] = jnp.transpose(taps_t[...]).reshape(planes, piece, TAPS)
    frecv[z] = fpart[z]

    for d in along_z:
        other, device = z_peer(d)
        push(RS, fpart.at[other], frecv.at[z], device)

    run(gated, SPAN, entering(ends_f, states_f, ST_F, False), False, emit_u)
    push(HALO_U, last_u, past_u, z_peer(1)[1])
    move_sublanes(u, SPAN, 0, 1)

    over_z, over_plane = pl.ds(0, half_piece), pl.ds(half_piece, half_piece)

    def sum_planes():
        await_bytes(recv.at[RS], frecv.at[pl.ds(0, planes - 1)])
        value = frecv[0]
        for other in range(1, planes):
            value = value + frecv[other]
        fmine[...] = value
        z_place, plane_place = fg_out.at[i, z, over_z], fg_out.at[i, z, over_plane]

        for d in along_z:
            push(Z1, fmine.at[over_z], z_place, z_peer(d)[1])

        for step in in_row:
            push(P1, fmine.at[over_plane], plane_place, row_peer(step)[1])

        keep(Z1, fmine.at[over_z], z_place)
        keep(P1, fmine.at[over_plane], plane_place)

    def spread():
        await_bytes(recv.at[P1], fg_out.at[:, 0, over_plane])

        for d in along_z:
            place = fg_out.at[:, z, over_plane]
            push(P2, place, place, z_peer(d)[1])

        await_bytes(recv.at[Z1], fg_out.at[0, :, over_z])

        for step in in_row:
            place = fg_out.at[i, :, over_z]
            push(Z2, place, place, row_peer(step)[1])

    await_bytes(recv.at[HALO_B], future)
    merge(sg, SPAN, future, SEGS - 1, z == planes - 1)
    differences(sg, 0, sg_s)
    ahead_products(0, 2 * TOP)
    sum_planes()
    recombine(store_mixed, (0,), False)
    output(OUT_KV0, (in_kv.at[1], in_kv.at[0]), mixed_n, out_kv, kvg_out, 0, HALF)
    ahead_products(2 * TOP, PARTS)
    recombine(store_mixed, (1,), False)
    output(OUT_KV1, (in_kv.at[1], in_kv.at[0]), mixed_n, out_kv, kvg_out, HALF, HALF)

    await_bytes(recv.at[HALO_U], past_u)
    merge(u, 0, past_u, 0, z == 0)
    differences(u, 1, gated_s)
    past_products(0, 2 * TOP)
    recombine(store_long, (0,), False)
    output(OUT_Q0, (in_qu.at[1],), long_n, out_q, qg_out, 0, HALF)
    past_products(2 * TOP, PARTS)
    recombine(store_long, (1,), False)
    output(OUT_Q1, (in_qu.at[1],), long_n, out_q, qg_out, HALF, HALF)
    spread()

    low, high = pl.ds(0, HALF), pl.ds(HALF, HALF)
    most, other_planes = pl.ds(0, SEGS - 1), pl.ds(0, planes - 1)
    for stage, like in ((QU, in_qu), (KV, in_kv)):
        await_bytes(send.at[stage], like.at[:, most])
        if parts > 1:
            await_bytes(send.at[stage], like.at[:, 0, pl.ds(0, SPAN - rows)])
    for stage, like in (
        (HALO_F, past),
        (HALO_B, future),
        (HALO_U, past_u),
        (ST_F, states_f.at[other_planes]),
        (ST_B, states_b.at[other_planes]),
        (RS, frecv.at[other_planes]),
        (Z1, fg_out.at[0, other_planes, over_z]),
        (P1, fg_out.at[most, 0, over_plane]),
        (OUT_KV0, out_kv.at[:, most, low]),
        (OUT_KV1, out_kv.at[:, most, high]),
        (OUT_Q0, out_q.at[:, most, low]),
        (OUT_Q1, out_q.at[:, most, high]),
        (Z2, fg_out.at[most, :, over_z]),
        (P2, fg_out.at[:, other_planes, over_plane]),
    ):
        await_bytes(send.at[stage], like)
    for stage, like in (
        (OUT_KV0, kvg_out.at[:, low]),
        (OUT_KV1, kvg_out.at[:, high]),
        (OUT_Q0, qg_out.at[:, low]),
        (OUT_Q1, qg_out.at[:, high]),
        (Z2, fg_out.at[most, :, over_z]),
        (P2, fg_out.at[:, other_planes, over_plane]),
    ):
        await_bytes(recv.at[stage], like)


def finish(q, kv, filt, q_result, k_result, v_result, filt_result, done):
    pairs = ((q.at[0], q_result), (kv.at[0], k_result), (kv.at[1], v_result), (filt, filt_result))
    copies = [
        pltpu.make_async_copy(src.at[rows], dst.at[rows], done.at[n, c])
        for n, (src, dst) in enumerate(pairs)
        for c, rows in enumerate(pl.ds(src.shape[0] // 4 * c, src.shape[0] // 4) for c in range(4))
    ]
    for copy in copies:
        copy.start()
    for copy in copies:
        copy.wait()


def body(planes, parts, q_gate, key_in, value_in, out_grad, mr_filter, residues, decay_rates):
    piece = TAPS // planes
    f32, bf16 = jnp.float32, jnp.bfloat16

    def vmem(*shape, kind=f32):
        return pltpu.VMEM(shape, kind)

    scratch = [
        vmem(4, *q_gate.shape, kind=bf16),
        vmem(2, SEGS, SPAN, LANES, kind=bf16),
        vmem(2, SEGS, SPAN, LANES, kind=bf16),
        vmem(LANES, TAPS),
        vmem(MODES, LANES),
        vmem(MODES, LANES),
        vmem(TAPS, LANES),
        vmem(PARTS, SUB, SEGS, LANES),
        vmem(MODES, SEGS, LANES),
        vmem(MODES, SEGS, LANES),
        vmem(SEGS * PITCH, LANES),
        vmem(2 * SPAN, SEGS, LANES),
        vmem(PARTS, 2 * SUB, SEGS, LANES),
        vmem(2 * SPAN, SEGS, LANES),
        vmem(SEGS * PITCH, LANES),
        vmem(SPAN, SEGS, LANES),
        vmem(MODES * SEGS, LANES),
        vmem(MODES * SEGS, LANES),
        vmem(MODES * SEGS, LANES),
        vmem(planes, MODES, LANES),
        vmem(planes, MODES, LANES),
        vmem(SEGS * PITCH, LANES),
        vmem(2 * SPAN, SEGS, LANES),
        vmem(PARTS, 2 * SUB, SEGS, LANES),
        vmem(PARTS, SUB, SEGS, LANES),
        vmem(SPAN, LANES),
        vmem(SPAN, LANES),
        vmem(SPAN, LANES),
        vmem(SPAN, LANES),
        vmem(SPAN, LANES),
        vmem(PARTS, SUB, SEGS, LANES),
        vmem(SEGS * PITCH, LANES),
        vmem(1, SEGS, SPAN, LANES, kind=bf16),
        vmem(2, SEGS, SPAN, LANES, kind=bf16),
        vmem(TAPS * SEGS, LANES),
        vmem(planes, piece, TAPS),
        vmem(planes, piece, TAPS),
        vmem(piece, TAPS),
        pltpu.SemaphoreType.DMA((STAGES,)),
        pltpu.SemaphoreType.DMA((STAGES,)),
        pltpu.SemaphoreType.DMA((7,)),
    ]
    anywhere = pl.BlockSpec(memory_space=pl.ANY)
    hbm = pl.BlockSpec(memory_space=pltpu.HBM)
    out = jax.ShapeDtypeStruct((SPAN, SEGS * LANES), bf16)
    filter_out = jax.ShapeDtypeStruct((SEGS, planes, piece, TAPS), f32)
    gathered = [jax.ShapeDtypeStruct((n, *out.shape), bf16) for n in (1, 2)] + [filter_out]
    operands = (q_gate, key_in, value_in, out_grad, mr_filter, residues.T, decay_rates.T)
    operands = [pltpu.with_memory_space_constraint(x, pltpu.HBM) for x in operands]
    results = pl.pallas_call(
        functools.partial(kernel, planes, parts),
        out_shape=tuple(pltpu.VMEM(x.shape, x.dtype) for x in gathered),
        in_specs=[hbm] * 7,
        out_specs=(anywhere,) * 3,
        scratch_shapes=scratch,
        compiler_params=pltpu.CompilerParams(
            collective_id=0, has_side_effects=True, vmem_limit_bytes=VMEM
        ),
    )(*operands)
    *grads, filter_grad = pl.pallas_call(
        finish,
        out_shape=tuple(pltpu.HBM(x.shape, x.dtype) for x in (out, out, out, filter_out)),
        in_specs=[anywhere] * 3,
        out_specs=(hbm,) * 4,
        scratch_shapes=[pltpu.SemaphoreType.DMA((4, 4))],
        compiler_params=pltpu.CompilerParams(vmem_limit_bytes=VMEM),
    )(*results)
    return (*grads, filter_grad.reshape(SEGS * LANES, TAPS))


def solution(mesh):
    rows = P(("seq", "tp"), None)
    return jax.shard_map(
        functools.partial(body, mesh.shape["seq"] // SEGS, mesh.shape["tp"]),
        mesh=mesh,
        in_specs=(rows, rows, rows, rows, P("tp", None), P("tp", None), P("tp", None)),
        out_specs=(P("seq", "tp"), P("seq", "tp"), P("seq", "tp"), P("tp", None)),
        check_vma=False,
    )
```
